128 devices in a mesh: dp: 16 (over y, z), ep: 8 (over x, core).
Axes of the slice: x: 4, y: 4, z: 4, core: 2. Of those that a mesh axis runs over, the one named last changes fastest.
Arguments:
- hidden: bfloat16 [2, 1024, 7168], P(None, ('dp', 'ep')), may hold values from -6 to 6
- expert_ids: int32 [2, 1024, 8], P(None, ('dp', 'ep')), may hold values from 0 to 31, all different within a row; in each aligned block of 8 rows (0 to 7, 8 to 15, ..., all dimensions but the last counted through in order) at most 3 rows name the same one
- expert_gates: float32 [2, 1024, 8], P(None, ('dp', 'ep')), may hold values from 0.1 to 0.6
- w_gate: bfloat16 [32, 7168, 1024], P('dp', 'ep'), may hold values from -0.0625 to 0.0625
- w_up: bfloat16 [32, 7168, 1024], P('dp', 'ep'), may hold values from -0.0625 to 0.0625
- w_down: bfloat16 [32, 1024, 7168], P('dp', None, 'ep'), may hold values from -0.1875 to 0.1875
- w_latent: bfloat16 [7168, 576], P('ep'), may hold values from -0.0625 to 0.0625
- queries: bfloat16 [2, 1024, 128, 576], P(None, ('dp', 'ep')), may hold values from -16 to 16
- cache: bfloat16 [1024, 512, 576], P(('dp', 'ep')), may hold values from -8 to 8
- lengths: int32 [1024], replicated, may hold values from 2 to 510
- came_from: int32 [1024], replicated, may hold values from 0 to 1023, as said below
Outputs:
- expert_out: bfloat16 [2, 1024, 7168], P(None, ('dp', 'ep'))
- attended: bfloat16 [2, 1024, 128, 512], P(None, ('dp', 'ep'))
The draws below stay inside these ranges and needn't reach their ends.
Inputs may be any that keep to these rules, and one draw needn't show every extreme that they name: `expert_ids`: in each step, no expert is picked by more than 3 of the 8 rows of one device, and the rows of one device pick distinct experts each. `came_from`: A permutation of the slots; a slot takes a row from a device with the same ep index; on every device exactly 2 rows leave and exactly 2 slots take a row from another device, never two from the same device.
All inputs are finite; a program needn't handle non-finite values.
Results may differ from the reference program's by a relative error of at most 0.0085.
Values may be sent and summed in bfloat16 or wider, within the bound.
No kernel may reach another device: no remote copies, remote signals or barrier semaphores. Data moves between devices by JAX's collectives and lax.ppermute only.
A program may use at most 128 MiB of HBM per device.

```python
import math
import jax
import jax.numpy as jnp
import numpy as np
from jax import lax

D = 7168
HEADS = 128
LAT = 512
EXP_FF = 1024
TOPK = 8
STEPS = 2
MOVE_DEV = 2
ROWS_DEV = 8
CACHE_CAP = 512
KV = 576
EXPERTS = 32
CAP = 3
ROWS_TOTAL = 1024
N_DP = 16
N_EP = 8


def migration_table(key):
    base = jax.random.fold_in(key, 71)
    first_key, second_key = jax.random.split(base)
    order = jax.vmap(lambda part_key: jax.random.permutation(part_key, N_DP))(jax.random.split(first_key, N_EP))
    movers = jax.vmap(lambda part_key: jax.random.permutation(part_key, ROWS_DEV)[:MOVE_DEV])(jax.random.split(second_key, N_DP * N_EP))
    movers = movers.reshape(N_DP, N_EP, MOVE_DEV)
    table = jnp.arange(ROWS_TOTAL, dtype=jnp.int32).reshape(N_DP, N_EP, ROWS_DEV)
    column = jnp.broadcast_to(jnp.arange(N_EP, dtype=jnp.int32)[:, None], (N_EP, N_DP))
    for shift in range(MOVE_DEV):
        target_dp = order
        source_dp = jnp.roll(order, 1 + shift, axis=1)
        target_slot = movers[target_dp, column, shift]
        source_slot = movers[source_dp, column, shift]
        source_global = (source_dp * N_EP + column) * ROWS_DEV + source_slot
        table = table.at[target_dp, column, target_slot].set(source_global.astype(jnp.int32))
    return table.reshape(ROWS_TOTAL).astype(jnp.int32)


def draw_came_from(key, part):
    table = migration_table(key)
    return table


def draw_lengths(key, part):
    key = jax.random.fold_in(key, 13)
    most = CACHE_CAP - 2
    devices = N_DP * N_EP
    long_dev = jax.random.randint(jax.random.fold_in(key, 1), (devices, 1), 0, 2)
    long_vals = jax.random.randint(jax.random.fold_in(key, 2), (devices, ROWS_DEV), most // 2, most + 1)
    short_vals = jax.random.randint(jax.random.fold_in(key, 3), (devices, ROWS_DEV), 2, most // 4 + 3)
    values = jnp.where(long_dev == 1, long_vals, short_vals).reshape(ROWS_TOTAL)
    chosen = jax.random.permutation(jax.random.fold_in(key, 4), ROWS_TOTAL)
    values = values.at[chosen[0]].set(most).at[chosen[1]].set(2)
    return values.astype(jnp.int32)


def draw_cache(key, part):
    key = jax.random.fold_in(key, 7)
    shape = (ROWS_TOTAL, CACHE_CAP, KV)
    values = jnp.clip(jax.random.normal(key, shape, jnp.float32), -6.0, 6.0)
    return values.astype(jnp.bfloat16)


def draw_queries(key, part):
    key = jax.random.fold_in(key, 9)
    values = jnp.clip(1.5 * jax.random.normal(key, (STEPS, ROWS_TOTAL, HEADS, KV), jnp.float32), -16.0, 16.0)
    return values.astype(jnp.bfloat16)


def shard_levels(stream_key, dims, pieces, low, high):
    loudness, own = 1.0, jax.random.fold_in(stream_key, 6)
    for axis_at, parts in pieces:
        heights = jnp.exp(jax.random.uniform(jax.random.fold_in(own, axis_at), (parts,), jnp.float32, low / len(pieces), high / len(pieces)))
        loudness = loudness * jnp.repeat(heights, dims[axis_at] // parts).reshape([-1 if axis == axis_at else 1 for axis in range(len(dims))])
    return loudness


def assign_block(stream_key, own, number, rows, amount, top, reach, skew):
    ranking = jax.random.permutation(stream_key, amount)
    heavy_load, ordinary = shares(amount, rows * top, reach, skew, True), shares(amount, rows * top, reach, skew, False)
    places = jnp.arange(amount)

    def named(tallies, offset_by):
        used = int((tallies > 0).sum())
        fixed = max(1, used // 4)
        shifted = fixed + (places - fixed + offset_by * (used - fixed)) % max(1, amount - fixed)
        return jnp.zeros((amount,), jnp.int32).at[ranking[jnp.where(places < fixed, places, shifted)]].set(jnp.asarray(tallies, jnp.int32))

    tallies = jnp.where(number % 4 == 0, named(heavy_load, number // 4), named(ordinary, number - number // 4 - 1))
    mixed = jax.random.permutation(jax.random.fold_in(own, 3), amount)
    source_of, taker = mixed[0:amount // 2 * 2:2], mixed[1:amount // 2 * 2:2]
    slack = jnp.minimum(tallies[source_of] - 1, reach - tallies[taker]) // 2
    slack = jnp.where((source_of == ranking[0]) | (taker == ranking[0]) | (tallies[taker] == 0), 0, jnp.maximum(slack, 0))
    shifted = jax.random.randint(jax.random.fold_in(own, 4), (amount // 2,), 0, 1 << 20) % (slack + 1)
    tallies = tallies.at[source_of].add(-shifted).at[taker].add(shifted)
    labels = jnp.searchsorted(jnp.cumsum(tallies), jnp.arange(rows * top), side="right").astype(jnp.int32)
    table = labels.reshape(top, rows).T
    table = table[jax.random.permutation(jax.random.fold_in(own, 1), rows)]
    offset_by = jax.random.randint(jax.random.fold_in(own, 2), (rows, 1), 0, top)
    return jnp.take_along_axis(table, (jnp.arange(top)[None, :] + offset_by) % top, axis=1)


def shares(number_of, total, limit, slope, full):
    portions = [(1 << 20) // math.isqrt(standing ** slope) + 1 for standing in range(1, number_of + 1)]
    largest = limit if full else min(limit, max(-(-total // number_of), total * portions[0] // sum(portions)))
    least = 1 if total - largest >= number_of - 1 else 0
    holding, rest = [largest] + [least] * (number_of - 1), total - largest - least * (number_of - 1)
    while rest > 0:
        free = [i for i in range(1, number_of) if holding[i] < largest] or [i for i in range(1, number_of) if holding[i] < limit]
        pool, budget = sum([portions[i] for i in free]), rest
        for i in free:
            more = min(limit - holding[i], max(1, budget * portions[i] // pool), rest)
            holding[i] = holding[i] + more
            rest = rest - more
    return np.array(holding)


def bell_draw(stream_key, dims, width, reach, shards=(), kind=jnp.bfloat16):
    factor_of = shard_levels(stream_key, dims, shards, -0.22, 0.18) if shards else 1.0
    drawn = jax.random.normal(stream_key, dims, jnp.float32) * width * factor_of
    return jnp.minimum(jnp.maximum(drawn, -reach), reach).astype(kind)


def setup_inputs(seed: int = 0) -> dict:
    splits = jax.random.split(jax.random.key(seed), 12)
    hidden = bell_draw(splits[0], (STEPS, ROWS_TOTAL, D), 1.0, 6.0, ((1, 128),))
    expert_ids_keys = jax.random.split(jax.random.fold_in(splits[1], 1), STEPS * ROWS_TOTAL // ROWS_DEV)
    expert_ids_turns = jax.random.permutation(jax.random.fold_in(splits[1], 3), STEPS * ROWS_TOTAL // ROWS_DEV)
    expert_ids = jax.vmap(lambda own, number: assign_block(jax.random.fold_in(splits[1], 2), own, number, ROWS_DEV, EXPERTS, TOPK, CAP, 2))(expert_ids_keys, expert_ids_turns).reshape((STEPS, ROWS_TOTAL, TOPK))
    expert_gates = jnp.clip(0.1 + 0.5 * jax.random.uniform(splits[2], (STEPS, ROWS_TOTAL, TOPK), jnp.float32) ** shard_levels(splits[2], (STEPS, ROWS_TOTAL, TOPK), ((1, 128),), -0.2, 0.2), 0.1, 0.6)
    w_gate = bell_draw(splits[3], (EXPERTS, D, EXP_FF), D ** -0.5, 0.0625, ((0, 16), (1, 8)))
    w_up = bell_draw(splits[4], (EXPERTS, D, EXP_FF), D ** -0.5, 0.0625, ((0, 16), (1, 8)))
    w_down = bell_draw(splits[5], (EXPERTS, EXP_FF, D), EXP_FF ** -0.5, 0.1875, ((0, 16), (2, 8)))
    w_latent = bell_draw(splits[6], (D, KV), D ** -0.5, 0.0625, ((0, 8),))
    queries = draw_queries(jax.random.fold_in(splits[11], 71), 0)
    cache = draw_cache(jax.random.fold_in(splits[11], 71), 0)
    lengths = draw_lengths(jax.random.fold_in(splits[11], 71), 0)
    came_from = draw_came_from(jax.random.fold_in(splits[11], 71), 0)
    return dict(hidden=hidden, expert_ids=expert_ids, expert_gates=expert_gates, w_gate=w_gate, w_up=w_up, w_down=w_down, w_latent=w_latent, queries=queries, cache=cache, lengths=lengths, came_from=came_from)


SCORE_SCALE = 192.0 ** (-0.5)
EPSILON = 1e-06

def row_norm(values):
    return values * lax.rsqrt(lax.optimization_barrier(jnp.mean(values * values, axis=-1, keepdims=True)) + EPSILON)

def rotate_half(part, position):
    half = part.shape[-1] // 2
    freq = 10000.0 ** (-2.0 * jnp.arange(half, dtype=jnp.float32) / part.shape[-1])
    angle = position.astype(jnp.float32)[:, None] * freq[None, :]
    cosine = jnp.cos(angle)
    sine = jnp.sin(angle)
    first = part[:, :half]
    second = part[:, half:]
    return jnp.concatenate([first * cosine - second * sine, second * cosine + first * sine], axis=1)

def make_key(kv_raw, position):
    latent = row_norm(kv_raw[:, :LAT])
    return jnp.concatenate([latent, rotate_half(kv_raw[:, LAT:], position)], axis=1).astype(jnp.bfloat16)

def place_key(keys, new_key, position):
    spot = jnp.arange(keys.shape[1], dtype=jnp.int32)[None, :] == position[:, None].astype(jnp.int32)
    return jnp.where(spot[:, :, None], new_key[:, None, :], keys)

def attend(queries, keys, count):
    scores = jnp.einsum('rhk,rck->rhc', queries.astype(jnp.float32), keys.astype(jnp.float32)) * SCORE_SCALE
    valid = jnp.arange(keys.shape[1], dtype=jnp.int32)[None, :] < count[:, None].astype(jnp.int32)
    scores = jnp.where(valid[:, None, :], scores, -jnp.inf)
    top = lax.optimization_barrier(jnp.max(scores, axis=2, keepdims=True))
    weights = jnp.exp(scores - top)
    probs = (weights / lax.optimization_barrier(jnp.sum(weights, axis=2, keepdims=True))).astype(jnp.bfloat16)
    values = keys[:, :, :LAT].astype(jnp.float32)
    return jnp.einsum('rhc,rcl->rhl', probs.astype(jnp.float32), values).astype(jnp.bfloat16)

def expert_step(hidden_rows, ids, gates, w_gate, w_up, w_down, w_latent):
    devices = N_DP * N_EP
    experts = w_gate.shape[0]
    start = hidden_rows.astype(jnp.float32)
    normed = row_norm(start).astype(jnp.bfloat16)
    flat = ids.reshape(devices, ROWS_DEV * TOPK).astype(jnp.int32)
    onehot = (flat[:, :, None] == jnp.arange(experts, dtype=jnp.int32)[None, None, :]).astype(jnp.int32)
    before = jnp.cumsum(onehot, axis=1) - onehot
    rank = lax.optimization_barrier(jnp.sum(before * onehot, axis=2)).astype(jnp.int32)
    position = (jnp.arange(devices, dtype=jnp.int32)[:, None] * CAP + rank).astype(jnp.int32)
    row_of = (jnp.arange(devices * ROWS_DEV * TOPK, dtype=jnp.int32) // TOPK).astype(jnp.int32)
    table = jnp.full((experts, devices * CAP), -1, jnp.int32)
    table = table.at[flat.reshape(-1), position.reshape(-1)].set(row_of)

    def one_expert(packed):
        rows, gate_w, up_w, down_w = packed
        taken = normed[jnp.maximum(rows, 0)]
        inputs = jnp.where((rows >= 0)[:, None], taken, jnp.zeros_like(taken))
        gate = jnp.dot(inputs, gate_w, preferred_element_type=jnp.float32)
        upper = jnp.dot(inputs, up_w, preferred_element_type=jnp.float32)
        act = (jax.nn.silu(gate) * upper).astype(jnp.bfloat16)
        return jnp.dot(act, down_w, preferred_element_type=jnp.float32).astype(jnp.bfloat16)
    results = lax.map(one_expert, (table, w_gate, w_up, w_down))
    picked = results[flat.reshape(-1), position.reshape(-1)].reshape(ROWS_TOTAL, TOPK, D)
    mixed = lax.optimization_barrier(jnp.sum(gates[:, :, None].astype(jnp.float32) * picked.astype(jnp.float32), axis=1))
    lat_in = row_norm(start + mixed).astype(jnp.bfloat16)
    kv_raw = jnp.dot(lat_in, w_latent, preferred_element_type=jnp.float32)
    return (mixed, kv_raw)

def reference(hidden, expert_ids, expert_gates, w_gate, w_up, w_down, w_latent, queries, cache, lengths, came_from):
    mixed_first, raw_first = expert_step(hidden[0], expert_ids[0], expert_gates[0], w_gate, w_up, w_down, w_latent)
    mixed_second, raw_second = expert_step(hidden[1], expert_ids[1], expert_gates[1], w_gate, w_up, w_down, w_latent)
    first_key = make_key(raw_first, lengths)
    second_len = lengths[came_from]
    second_key = make_key(raw_second, second_len + 1)
    blocks = ROWS_TOTAL // ROWS_DEV

    def first_block(index):
        begin = (index * ROWS_DEV).astype(jnp.int32)
        keys = place_key(lax.dynamic_slice_in_dim(cache, begin, ROWS_DEV, 0), lax.dynamic_slice_in_dim(first_key, begin, ROWS_DEV, 0), lax.dynamic_slice_in_dim(lengths, begin, ROWS_DEV, 0))
        count = lax.dynamic_slice_in_dim(lengths, begin, ROWS_DEV, 0) + 1
        return attend(lax.dynamic_slice_in_dim(queries[0], begin, ROWS_DEV, 0), keys, count)

    def second_block(index):
        begin = (index * ROWS_DEV).astype(jnp.int32)
        source = lax.dynamic_slice_in_dim(came_from, begin, ROWS_DEV, 0)
        old_len = lengths[source]
        keys = place_key(cache[source], first_key[source], old_len)
        keys = place_key(keys, lax.dynamic_slice_in_dim(second_key, begin, ROWS_DEV, 0), old_len + 1)
        return attend(lax.dynamic_slice_in_dim(queries[1], begin, ROWS_DEV, 0), keys, old_len + 2)
    order = jnp.arange(blocks, dtype=jnp.int32)
    first_out = lax.map(first_block, order).reshape(ROWS_TOTAL, HEADS, LAT)
    second_out = lax.map(second_block, order).reshape(ROWS_TOTAL, HEADS, LAT)
    expert_out = jnp.stack([mixed_first, mixed_second]).astype(jnp.bfloat16)
    attended = jnp.stack([first_out, second_out])
    return (expert_out, attended)
```

```python
import functools

import jax
import jax.numpy as jnp
from jax import lax
from jax.experimental import pallas as pl
from jax.experimental.pallas import tpu as pltpu
from jax.sharding import PartitionSpec as P

F32 = jnp.float32
BF16 = jnp.bfloat16
D = 7168
LAT = 512
KV = 576
FF = 1024
EXPERTS = 32
CAP = 3
N_DP = 16
N_EP = 8
SLICE = D // N_EP
META = 128
WIDE = SLICE + META
ROWS = 8
TOPK = 8
SLOTS = EXPERTS * CAP * N_EP
PER_DP = SLOTS // N_DP
HALF = SLOTS // 2
KVW = 768
KEYW = 640
SCALE = 192.0 ** (-0.5)
EPS = 1e-06
VMEM = pl.BlockSpec(memory_space=pltpu.VMEM)
ANY = pl.BlockSpec(memory_space=pl.ANY)
PARAMS = pltpu.CompilerParams(vmem_limit_bytes=48 * 1024 * 1024)


def cost(flops, nbytes):
    return pl.CostEstimate(flops=int(flops), bytes_accessed=int(nbytes), transcendentals=0)


def split3(v):
    hi = v.astype(BF16).astype(F32)
    mid = (v - hi).astype(BF16).astype(F32)
    lo = (v - hi - mid).astype(BF16).astype(F32)
    return hi, mid, lo


def pack_kernel(hidden_ref, ids_ref, gates_ref, out_ref):
    lane = lax.broadcasted_iota(jnp.int32, (ROWS, META), 1)
    rows = []
    metas = []
    for s in range(2):
        h = hidden_ref[s].astype(F32)
        scale = lax.rsqrt(jnp.mean(h * h, axis=-1, keepdims=True) + EPS)
        ids = ids_ref[s].astype(F32)
        parts = split3(gates_ref[s])
        meta = jnp.zeros((ROWS, META), F32)
        for k in range(TOPK):
            meta = jnp.where(lane == k, ids[:, k : k + 1], meta)
            for n, part in enumerate(parts):
                meta = jnp.where(lane == 8 + 8 * n + k, part[:, k : k + 1], meta)
        for n, part in enumerate(split3(scale)):
            meta = jnp.where(lane == 32 + n, part, meta)
        rows.append(h)
        metas.append(meta)
    meta = jnp.concatenate(metas, axis=0).astype(BF16)
    for j in range(N_EP):
        cut = slice(j * SLICE, (j + 1) * SLICE)
        both = jnp.concatenate([rows[0][:, cut], rows[1][:, cut]], axis=0)
        out_ref[j, :, :SLICE] = both.astype(BF16)
        out_ref[j, :, SLICE:] = meta


def unpack(r_ref, s):
    rows = r_ref[...].astype(F32)[:, 8 * s : 8 * s + 8, :].reshape(N_EP * ROWS, WIDE)
    n = N_EP * ROWS
    hid = rows[:, :SLICE]
    meta = rows[:, SLICE:]
    mt = meta.T
    ids = mt[0:8]
    gates = mt[8:16] + mt[16:24] + mt[24:32]
    scale = meta[:, 32:33] + meta[:, 33:34] + meta[:, 34:35]
    expert = lax.broadcasted_iota(jnp.int32, (EXPERTS, n), 0).astype(F32)
    onehot = jnp.zeros((EXPERTS, n), F32)
    gm = jnp.zeros((EXPERTS, n), F32)
    for k in range(TOPK):
        eq = expert == ids[k : k + 1]
        onehot = jnp.where(eq, 1.0, onehot)
        gm = jnp.where(eq, gates[k : k + 1], gm)
    p = lax.broadcasted_iota(jnp.int32, (n, n), 0)
    q = lax.broadcasted_iota(jnp.int32, (n, n), 1)
    earlier = jnp.where(((p >> 3) == (q >> 3)) & (p < q), 1.0, 0.0).astype(BF16)
    rank = jnp.dot(onehot.astype(BF16), earlier, preferred_element_type=F32)
    b = lax.broadcasted_iota(jnp.int32, (N_EP, n), 0)
    qq = lax.broadcasted_iota(jnp.int32, (N_EP, n), 1)
    block = jnp.where((qq >> 3) == b, 1.0, 0.0)

    def place(values):
        pieces = []
        for r in range(CAP):
            picked = jnp.where((rank == float(r)) & (onehot > 0.0), values, 0.0)
            pieces.append((picked[:, None, :] * block[None, :, :])[:, None])
        return jnp.concatenate(pieces, axis=1).reshape(SLOTS, n)

    return hid, scale, onehot, gm, place


def dispatch_kernel(r_ref, out0_ref, out1_ref):
    for s, out_ref in enumerate((out0_ref, out1_ref)):
        hid, scale, onehot, _, place = unpack(r_ref, s)
        normed = (hid * scale).astype(BF16)
        table = place(onehot).astype(BF16)
        out = jnp.dot(table, normed, preferred_element_type=F32)
        out_ref[...] = out.reshape(N_DP, PER_DP, SLICE).astype(BF16)


def gateup_kernel(at_ref, x_ref, wg_ref, wu_ref, keep_ref, send_ref):
    core = at_ref[1]
    for e in range(2):
        lhs = x_ref[:, 16 * e : 16 * e + 32, :].reshape(N_DP * 32, SLICE)
        halves = []
        for w_ref in (wg_ref, wu_ref):
            full = jnp.dot(lhs, w_ref[e], preferred_element_type=F32)
            full = full.reshape(N_DP, 32, 256)[:, 8 * e : 8 * e + 24, :].reshape(HALF, 256)
            halves.append((full[:, :128], full[:, 128:]))
        (g0, g1), (u0, u1) = halves
        first = core == 0
        keep_ref[0, e, :, :128] = jnp.where(first, g0, g1).astype(BF16)
        keep_ref[0, e, :, 128:] = jnp.where(first, u0, u1).astype(BF16)
        send_ref[0, e, :, :128] = jnp.where(first, g1, g0).astype(BF16)
        send_ref[0, e, :, 128:] = jnp.where(first, u1, u0).astype(BF16)


def gate_up(at, x, w_gate, w_up):
    wspec = pl.BlockSpec((2, SLICE, 256), lambda r, a: (0, 0, (a[0] + r) % 4))
    ospec = pl.BlockSpec((1, 2, HALF, 256), lambda r, a: (r, 0, 0, 0))
    shape = jax.ShapeDtypeStruct((4, 2, HALF, 256), BF16)
    return pl.pallas_call(
        gateup_kernel,
        grid_spec=pltpu.PrefetchScalarGridSpec(
            num_scalar_prefetch=1,
            grid=(4,),
            in_specs=[
                pl.BlockSpec((N_DP, PER_DP, SLICE), lambda r, a: (0, 0, 0)),
                wspec,
                wspec,
            ],
            out_specs=[ospec, ospec],
        ),
        out_shape=[shape, shape],
        compiler_params=PARAMS,
        cost_estimate=cost(4e9, 12e6),
        name="gate_up",
    )(at, x, w_gate, w_up)


def down_kernel(at_ref, *refs):
    acts = refs[:8]
    w_ref = refs[8]
    out_ref = refs[9]
    x = at_ref[0]
    first = at_ref[1] == 0
    results = []
    for e in range(2):
        total = jnp.zeros((HALF, SLICE), F32)
        for n, shift in enumerate((0, 3, 1, 2)):
            own = acts[n][e]
            other = acts[4 + n][e]
            low = jnp.where(first, own, other)
            high = jnp.where(first, other, own)
            lhs = jnp.concatenate([low, high], axis=1)
            chip = (x + shift) & 3
            rhs = w_ref[e, pl.ds(pl.multiple_of(chip * 256, 256), 256), :]
            total = total + jnp.dot(lhs, rhs, preferred_element_type=F32)
        results.append(total.reshape(N_DP, PER_DP // 2, SLICE))
    out_ref[...] = jnp.concatenate(results, axis=1).astype(BF16)


def down(at, acts, w_down):
    return pl.pallas_call(
        down_kernel,
        in_specs=[pl.BlockSpec(memory_space=pltpu.SMEM)] + [VMEM] * 9,
        out_specs=VMEM,
        out_shape=jax.ShapeDtypeStruct((N_DP, PER_DP, SLICE), BF16),
        compiler_params=PARAMS,
        cost_estimate=cost(2e9, 8e6),
        name="down",
    )(at, *acts, w_down)


def combine_kernel(s, r_ref, ret_ref, wl_ref, out_ref):
    hid, _, _, gm, place = unpack(r_ref, s)
    weights = place(gm)
    high = weights.astype(BF16)
    low = (weights - high.astype(F32)).astype(BF16)
    ret = ret_ref[...].reshape(SLOTS, SLICE)
    dims = (((0,), (0,)), ((), ()))
    mixed = lax.dot_general(high, ret, dims, preferred_element_type=F32)
    mixed = mixed + lax.dot_general(low, ret, dims, preferred_element_type=F32)
    resid = hid + mixed
    square = jnp.sum(resid * resid, axis=-1, keepdims=True)
    kv = lax.dot_general(
        resid.astype(BF16), wl_ref[...], (((1,), (1,)), ((), ())), preferred_element_type=F32
    )
    out_ref[:, :, :KV] = kv.reshape(N_EP, ROWS, KV)
    out_ref[:, :, KEYW:KVW] = jnp.broadcast_to(square, (N_EP * ROWS, KVW - KEYW)).reshape(
        N_EP, ROWS, KVW - KEYW
    )
    out_ref[:, :, KV:KEYW] = jnp.zeros((N_EP, ROWS, KEYW - KV), F32)
    out_ref[:, :, KVW:] = mixed.reshape(N_EP, ROWS, SLICE)


def key_kernel(z_ref, cos_ref, sin_ref, key_ref, mixed_ref):
    kv = jnp.sum(z_ref[:, :, :KVW], axis=0)
    for j in range(N_EP):
        mixed_ref[:, j * SLICE : (j + 1) * SLICE] = z_ref[j, :, KVW:].astype(BF16)
    raw = kv[:, :KEYW] * lax.rsqrt(kv[:, KEYW : KEYW + 1] * (1.0 / D) + EPS)
    latent = raw[:, :LAT]
    latent = latent * lax.rsqrt(jnp.mean(latent * latent, axis=-1, keepdims=True) + EPS)
    part = raw[:, LAT:]
    lane = lax.broadcasted_iota(jnp.int32, part.shape, 1)
    turned = jnp.where(lane < 32, -pltpu.roll(part, 96, 1), pltpu.roll(part, 32, 1))
    rotated = part * cos_ref[...] + turned * sin_ref[...]
    key_ref[:, :LAT] = latent.astype(BF16)
    key_ref[:, LAT:] = rotated.astype(BF16)


def old_attention(q, kt, count):
    scores = lax.dot_general(q, kt, (((0,), (0,)), ((), ())), preferred_element_type=F32) * SCALE
    lane = lax.broadcasted_iota(jnp.int32, scores.shape, 1)
    valid = lane < count
    scores = jnp.where(valid, scores, -1e30)
    top = jnp.max(scores, axis=1, keepdims=True)
    weights = jnp.where(valid, jnp.exp(scores - top), 0.0)
    total = jnp.sum(weights, axis=1, keepdims=True)
    out = lax.dot_general(
        weights.astype(BF16), kt[:LAT], (((1,), (1,)), ((), ())), preferred_element_type=F32
    )
    return out, top, total


def store_old(out_ref, stat_ref, parts):
    out, top, total = parts
    lane = lax.broadcasted_iota(jnp.int32, (128, 128), 1)
    out_ref[0] = out
    stat_ref[0] = jnp.where(lane == 0, top, total)


def old0_kernel(len_ref, q_ref, kt_ref, out_ref, stat_ref):
    count = len_ref[pl.program_id(0)]
    store_old(out_ref, stat_ref, old_attention(q_ref[0, 0], kt_ref[0], count))


def old1_kernel(tab_ref, q_ref, kt_ref, mig_ref, out_ref, stat_ref):
    t = pl.program_id(0)
    count = tab_ref[t]
    away = tab_ref[24 + t]

    @pl.when(away == 0)
    def _():
        store_old(out_ref, stat_ref, old_attention(q_ref[0, 0], kt_ref[0], count))

    @pl.when(away != 0)
    def _():
        store_old(out_ref, stat_ref, old_attention(q_ref[0, 0], mig_ref[0], count))


OLD_SHAPE = [
    jax.ShapeDtypeStruct((ROWS, 128, LAT), F32),
    jax.ShapeDtypeStruct((ROWS, 128, 128), F32),
]
OLD_SPECS = [
    pl.BlockSpec((1, 128, LAT), lambda t, a: (t, 0, 0)),
    pl.BlockSpec((1, 128, 128), lambda t, a: (t, 0, 0)),
]


def old0(lens, qt, cache_t):
    return pl.pallas_call(
        old0_kernel,
        grid_spec=pltpu.PrefetchScalarGridSpec(
            num_scalar_prefetch=1,
            grid=(ROWS,),
            in_specs=[
                pl.BlockSpec((1, 1, KV, 128), lambda t, a: (0, t, 0, 0)),
                pl.BlockSpec((1, KV, 512), lambda t, a: (t, 0, 0)),
            ],
            out_specs=OLD_SPECS,
        ),
        out_shape=OLD_SHAPE,
        compiler_params=PARAMS,
        cost_estimate=cost(5e9, 8e6),
        name="old0",
    )(lens, qt, cache_t)


def old1(table, qt, cache_t, moved):
    return pl.pallas_call(
        old1_kernel,
        grid_spec=pltpu.PrefetchScalarGridSpec(
            num_scalar_prefetch=1,
            grid=(ROWS,),
            in_specs=[
                pl.BlockSpec((1, 1, KV, 128), lambda t, a: (1, t, 0, 0)),
                pl.BlockSpec((1, KV, 512), lambda t, a: (a[8 + t], 0, 0)),
                pl.BlockSpec((1, KV, 512), lambda t, a: (a[16 + t], 0, 0)),
            ],
            out_specs=OLD_SPECS,
        ),
        out_shape=OLD_SHAPE,
        compiler_params=PARAMS,
        cost_estimate=cost(5e9, 8e6),
        name="old1",
    )(table, qt, cache_t, moved)


def merge_kernel(n_new, q_ref, old_ref, stat_ref, *refs):
    keys = refs[:n_new]
    out_ref = refs[-1]
    t = pl.program_id(0)
    lane = lax.broadcasted_iota(jnp.int32, (128, ROWS), 1)
    sub = lax.broadcasted_iota(jnp.int32, (ROWS, LAT), 0)
    top = stat_ref[0, :, 0:1]
    total = stat_ref[0, :, 1:2]
    q = q_ref[0, 0]
    scores = []
    values = []
    for key_ref in keys:
        both = lax.dot_general(
            q, key_ref[:, :KV], (((0,), (1,)), ((), ())), preferred_element_type=F32
        )
        scores.append(jnp.sum(jnp.where(lane == t, both, 0.0), axis=1, keepdims=True) * SCALE)
        latent = key_ref[:, :LAT].astype(F32)
        values.append(jnp.sum(jnp.where(sub == t, latent, 0.0), axis=0, keepdims=True))
    peak = top
    for s in scores:
        peak = jnp.maximum(peak, s)
    shrink = jnp.exp(top - peak)
    out = old_ref[0] * shrink
    total = total * shrink
    for s, v in zip(scores, values):
        w = jnp.exp(s - peak)
        total = total + w
        out = out + w * v
    out_ref[0, 0] = (out / total).astype(BF16)


def merge(step, qt, old, keys, buffer):
    n_new = len(keys)
    in_specs = [
        pl.BlockSpec((1, 1, KV, 128), lambda t: (step, t, 0, 0)),
        pl.BlockSpec((1, 128, LAT), lambda t: (t, 0, 0)),
        pl.BlockSpec((1, 128, 128), lambda t: (t, 0, 0)),
    ] + [pl.BlockSpec((ROWS, KEYW), lambda t: (0, 0))] * n_new
    args = [qt, *old, *keys]
    alias = {}
    if buffer is not None:
        in_specs.append(ANY)
        alias = {len(args): 0}
        args.append(buffer)
    return pl.pallas_call(
        functools.partial(merge_kernel, n_new),
        grid=(ROWS,),
        in_specs=in_specs,
        out_specs=pl.BlockSpec((1, 1, 128, LAT), lambda t: (step, t, 0, 0)),
        out_shape=jax.ShapeDtypeStruct((2, ROWS, 128, LAT), BF16),
        input_output_aliases=alias,
        compiler_params=PARAMS,
        cost_estimate=cost(1e8, 5e6),
        name="merge%d" % step,
    )(*args)


def forward_kernel(idx_ref, src_ref, out_ref, sem):
    copies = [
        pltpu.make_async_copy(src_ref.at[idx_ref[n]], out_ref.at[n], sem.at[n]) for n in range(2 * N_DP)
    ]
    for c in copies:
        c.start()
    for c in copies:
        c.wait()


def forward(idx, pieces):
    return pl.pallas_call(
        forward_kernel,
        in_specs=[pl.BlockSpec(memory_space=pltpu.SMEM), ANY],
        out_specs=ANY,
        out_shape=jax.ShapeDtypeStruct(pieces.shape, BF16),
        scratch_shapes=[pltpu.SemaphoreType.DMA((2 * N_DP,))],
        compiler_params=PARAMS,
        cost_estimate=cost(1e6, 3e6),
        name="forward",
    )(idx, pieces)


SIB = [(i, i ^ 1) for i in range(8)]
XP = [(i, (i + 2) % 8) for i in range(8)]
XM = [(i, (i - 2) % 8) for i in range(8)]
X2 = [(i, (i + 4) % 8) for i in range(8)]


def hop(v, pairs):
    return lax.ppermute(v, "ep", pairs)


def experts(at, arrived, w_gate, w_up, w_down):
    keep, send = gate_up(at, arrived, w_gate, w_up)
    got = hop(send, SIB)
    s1 = (keep[1].astype(F32) + got[1].astype(F32)).astype(BF16)
    s2 = (keep[2].astype(F32) + got[2].astype(F32)).astype(BF16)
    s3 = (keep[3].astype(F32) + got[3].astype(F32)).astype(BF16)
    a1 = hop(s1, XP)
    a2 = hop(s2, X2)
    a3 = hop(s3, XM)
    total = (
        keep[0].astype(F32)
        + got[0].astype(F32)
        + a1.astype(F32)
        + a2.astype(F32)
        + a3.astype(F32)
    )
    act = (jax.nn.silu(total[..., :128]) * total[..., 128:]).astype(BF16)
    b1 = hop(act, XP)
    b3 = hop(act, XM)
    b2 = hop(act, X2)
    own = [act, b1, b3, b2]
    other = [hop(v, SIB) for v in own]
    return down(at, own + other, w_down)


def local(
    hidden,
    expert_ids,
    expert_gates,
    w_gate,
    w_up,
    w_down,
    w_latent,
    queries,
    cache,
    lengths,
    came_from,
):
    my_dp = lax.axis_index("dp")
    my_ep = lax.axis_index("ep")
    my_dev = my_dp * N_EP + my_ep
    at = jnp.stack([my_ep // 2, my_ep % 2]).astype(jnp.int32)
    qt = jnp.swapaxes(queries, 2, 3)
    cache_t = jnp.swapaxes(cache, 1, 2)
    latent_t = w_latent.T

    packed = pl.pallas_call(
        pack_kernel,
        in_specs=[VMEM] * 3,
        out_specs=VMEM,
        out_shape=jax.ShapeDtypeStruct((N_EP, 2 * ROWS, WIDE), BF16),
        compiler_params=PARAMS,
        name="pack",
    )(hidden, expert_ids, expert_gates)
    gathered = lax.all_to_all(packed, "ep", split_axis=0, concat_axis=0, tiled=True)
    out_shape = jax.ShapeDtypeStruct((N_DP, PER_DP, SLICE), BF16)
    sends = pl.pallas_call(
        dispatch_kernel,
        in_specs=[VMEM],
        out_specs=[VMEM, VMEM],
        out_shape=[out_shape, out_shape],
        compiler_params=PARAMS,
        name="dispatch",
    )(gathered)

    table = lax.dynamic_index_in_dim(
        came_from.reshape(N_DP, N_EP, ROWS), my_ep, 1, keepdims=False
    )
    src_dp = table // (N_EP * ROWS)
    src_row = table % ROWS
    src_flat = (src_dp * ROWS + src_row).reshape(N_DP * ROWS)
    flat = lax.iota(jnp.int32, N_DP * ROWS)
    hit = src_flat[:, None] == flat[None, :]
    crosses = (flat // ROWS)[:, None] != (flat // ROWS)[None, :]
    away = jnp.any(hit & crosses, axis=0).reshape(N_DP, ROWS).astype(jnp.int32)
    rows_before = lax.iota(jnp.int32, ROWS)[:, None] < lax.iota(jnp.int32, ROWS)[None, :]
    label = jnp.sum(away[:, :, None] * rows_before[None], axis=1)
    label_of = jnp.sum(jnp.where(hit, label.reshape(1, -1), 0), axis=1).reshape(N_DP, ROWS)
    arriving = (src_dp != lax.iota(jnp.int32, N_DP)[:, None]).astype(jnp.int32)
    turn = jnp.sum(arriving[:, :, None] * rows_before[None], axis=1)
    source = src_dp * 2 + label_of
    pick = (turn[:, :, None] == lax.iota(jnp.int32, 2)) & (arriving[:, :, None] == 1)
    forward_idx = jnp.sum(jnp.where(pick, source[:, :, None], 0), axis=1).reshape(2 * N_DP)
    my_away = lax.dynamic_index_in_dim(away, my_dp, 0, keepdims=False)
    my_label = lax.dynamic_index_in_dim(label, my_dp, 0, keepdims=False)
    leave = (my_label[:, None] == lax.iota(jnp.int32, 2)) & (my_away[:, None] == 1)
    leaving = jnp.sum(jnp.where(leave, lax.iota(jnp.int32, ROWS)[:, None], 0), axis=0)
    my_src = lax.dynamic_index_in_dim(table, my_dp, 0, keepdims=False)
    my_src_flat = lax.dynamic_index_in_dim(
        src_flat.reshape(N_DP, ROWS), my_dp, 0, keepdims=False
    )
    my_arriving = lax.dynamic_index_in_dim(arriving, my_dp, 0, keepdims=False)
    my_turn = lax.dynamic_index_in_dim(turn, my_dp, 0, keepdims=False)
    own_len = lax.dynamic_slice_in_dim(lengths, my_dev * ROWS, ROWS)
    second_len = jnp.take(lengths, my_src)
    old_table = jnp.concatenate(
        [
            second_len,
            jnp.where(my_arriving == 1, 0, my_src % ROWS),
            jnp.where(my_arriving == 1, my_turn, 0),
            my_arriving,
        ]
    ).astype(jnp.int32)

    first_old = old0(own_len, qt, cache_t)

    two = jnp.concatenate(
        [lax.dynamic_slice_in_dim(cache_t, leaving[n], 1, 0) for n in range(2)], axis=0
    )
    pieces = two.reshape(2, 8, 72, 2, 256).transpose(1, 3, 0, 2, 4).reshape(N_DP, 2, 72, 256)
    spread = lax.all_to_all(pieces, "dp", split_axis=0, concat_axis=0, tiled=True)
    onward = forward(forward_idx, spread.reshape(2 * N_DP, 72, 256))

    positions = jnp.stack([own_len, second_len + 1]).astype(F32)
    freq = 10000.0 ** (-2.0 * jnp.arange(32, dtype=F32) / 64)
    angle = positions[:, :, None] * jnp.tile(freq, 4)[None, None, :]
    keep = jnp.arange(128) < 64
    cosine = jnp.where(keep, jnp.cos(angle), 0.0)
    sine = jnp.where(keep, jnp.sin(angle), 0.0)

    keys = []
    mixes = []
    arrived = [
        lax.all_to_all(sends[s], "dp", split_axis=0, concat_axis=0, tiled=True) for s in range(2)
    ]
    landed = lax.all_to_all(
        onward.reshape(N_DP, 2, 72, 256), "dp", split_axis=0, concat_axis=0, tiled=True
    )
    moved = landed.reshape(8, 2, 2, 72, 256).transpose(2, 0, 3, 1, 4).reshape(2, KV, 512)
    second_old = old1(old_table, qt, cache_t, moved)
    for s in range(2):
        result = experts(at, arrived[s], w_gate, w_up, w_down)
        returned = lax.all_to_all(result, "dp", split_axis=0, concat_axis=0, tiled=True)
        partial = pl.pallas_call(
            functools.partial(combine_kernel, s),
            in_specs=[VMEM] * 3,
            out_specs=VMEM,
            out_shape=jax.ShapeDtypeStruct((N_EP, ROWS, KVW + SLICE), F32),
            compiler_params=PARAMS,
            cost_estimate=cost(4e8, 4e6),
            name="combine%d" % s,
        )(gathered, returned, latent_t)
        summed = lax.all_to_all(partial, "ep", split_axis=0, concat_axis=0, tiled=True)
        key, mixed = pl.pallas_call(
            key_kernel,
            in_specs=[VMEM] * 3,
            out_specs=[VMEM, VMEM],
            out_shape=[
                jax.ShapeDtypeStruct((ROWS, KEYW), BF16),
                jax.ShapeDtypeStruct((ROWS, D), BF16),
            ],
            compiler_params=PARAMS,
            name="key%d" % s,
        )(summed, cosine[s], sine[s])
        keys.append(key)
        mixes.append(mixed)
    attended = merge(0, qt, first_old, [keys[0]], None)
    everyone = lax.all_to_all(
        jnp.broadcast_to(keys[0][None], (N_DP, ROWS, KEYW)),
        "dp",
        split_axis=0,
        concat_axis=0,
        tiled=True,
    ).reshape(N_DP * ROWS, KEYW)
    select = (my_src_flat[:, None] == flat[None, :]).astype(BF16)
    first_for_second = jnp.dot(select, everyone, preferred_element_type=F32).astype(BF16)
    attended = merge(1, qt, second_old, [first_for_second, keys[1]], attended)
    expert_out = jnp.stack(mixes)
    return (expert_out, attended)


def solution(mesh):
    in_specs = (
        P(None, ("dp", "ep"), None),
        P(None, ("dp", "ep"), None),
        P(None, ("dp", "ep"), None),
        P("dp", "ep", None),
        P("dp", "ep", None),
        P("dp", None, "ep"),
        P("ep", None),
        P(None, ("dp", "ep"), None, None),
        P(("dp", "ep"), None, None),
        P(),
        P(),
    )
    out_specs = (P(None, ("dp", "ep"), None), P(None, ("dp", "ep"), None, None))
    return jax.shard_map(local, mesh=mesh, in_specs=in_specs, out_specs=out_specs, check_vma=False)
```

```python
import functools

import jax
import jax.numpy as jnp
from jax import lax
from jax.experimental import pallas as pl
from jax.experimental.pallas import tpu as pltpu
from jax.sharding import PartitionSpec as P

F32 = jnp.float32
BF16 = jnp.bfloat16
D = 7168
LAT = 512
KV = 576
FF = 1024
EXPERTS = 32
CAP = 3
N_DP = 16
N_EP = 8
SLICE = D // N_EP
META = 128
WIDE = SLICE + META
ROWS = 8
TOPK = 8
SLOTS = EXPERTS * CAP * N_EP
PER_DP = SLOTS // N_DP
HALF = SLOTS // 2
KVW = 768
KEYW = 640
SCALE = 192.0 ** (-0.5)
EPS = 1e-06
VMEM = pl.BlockSpec(memory_space=pltpu.VMEM)
ANY = pl.BlockSpec(memory_space=pl.ANY)
PARAMS = pltpu.CompilerParams(vmem_limit_bytes=48 * 1024 * 1024)


def cost(flops, nbytes):
    return pl.CostEstimate(flops=int(flops), bytes_accessed=int(nbytes), transcendentals=0)


def split3(v):
    hi = v.astype(BF16).astype(F32)
    mid = (v - hi).astype(BF16).astype(F32)
    lo = (v - hi - mid).astype(BF16).astype(F32)
    return hi, mid, lo


def pack_kernel(hidden_ref, ids_ref, gates_ref, out_ref):
    lane = lax.broadcasted_iota(jnp.int32, (ROWS, META), 1)
    rows = []
    metas = []
    for s in range(2):
        h = hidden_ref[s].astype(F32)
        scale = lax.rsqrt(jnp.mean(h * h, axis=-1, keepdims=True) + EPS)
        ids = ids_ref[s].astype(F32)
        parts = split3(gates_ref[s])
        meta = jnp.zeros((ROWS, META), F32)
        for k in range(TOPK):
            meta = jnp.where(lane == k, ids[:, k : k + 1], meta)
            for n, part in enumerate(parts):
                meta = jnp.where(lane == 8 + 8 * n + k, part[:, k : k + 1], meta)
        for n, part in enumerate(split3(scale)):
            meta = jnp.where(lane == 32 + n, part, meta)
        rows.append(h)
        metas.append(meta)
    meta = jnp.concatenate(metas, axis=0).astype(BF16)
    for j in range(N_EP):
        cut = slice(j * SLICE, (j + 1) * SLICE)
        both = jnp.concatenate([rows[0][:, cut], rows[1][:, cut]], axis=0)
        out_ref[j, :, :SLICE] = both.astype(BF16)
        out_ref[j, :, SLICE:] = meta


def unpack(r_ref, s):
    rows = r_ref[...].astype(F32)[:, 8 * s : 8 * s + 8, :].reshape(N_EP * ROWS, WIDE)
    n = N_EP * ROWS
    hid = rows[:, :SLICE]
    meta = rows[:, SLICE:]
    mt = meta.T
    ids = mt[0:8]
    gates = mt[8:16] + mt[16:24] + mt[24:32]
    scale = meta[:, 32:33] + meta[:, 33:34] + meta[:, 34:35]
    expert = lax.broadcasted_iota(jnp.int32, (EXPERTS, n), 0).astype(F32)
    onehot = jnp.zeros((EXPERTS, n), F32)
    gm = jnp.zeros((EXPERTS, n), F32)
    for k in range(TOPK):
        eq = expert == ids[k : k + 1]
        onehot = jnp.where(eq, 1.0, onehot)
        gm = jnp.where(eq, gates[k : k + 1], gm)
    p = lax.broadcasted_iota(jnp.int32, (n, n), 0)
    q = lax.broadcasted_iota(jnp.int32, (n, n), 1)
    earlier = jnp.where(((p >> 3) == (q >> 3)) & (p < q), 1.0, 0.0).astype(BF16)
    rank = jnp.dot(onehot.astype(BF16), earlier, preferred_element_type=F32)
    b = lax.broadcasted_iota(jnp.int32, (N_EP, n), 0)
    qq = lax.broadcasted_iota(jnp.int32, (N_EP, n), 1)
    block = jnp.where((qq >> 3) == b, 1.0, 0.0)

    def place(values):
        pieces = []
        for r in range(CAP):
            picked = jnp.where((rank == float(r)) & (onehot > 0.0), values, 0.0)
            pieces.append((picked[:, None, :] * block[None, :, :])[:, None])
        return jnp.concatenate(pieces, axis=1).reshape(SLOTS, n)

    return hid, scale, onehot, gm, place


def dispatch_kernel(r_ref, out0_ref, out1_ref):
    for s, out_ref in enumerate((out0_ref, out1_ref)):
        hid, scale, onehot, _, place = unpack(r_ref, s)
        normed = (hid * scale).astype(BF16)
        table = place(onehot).astype(BF16)
        out = jnp.dot(table, normed, preferred_element_type=F32)
        out_ref[...] = out.reshape(N_DP, PER_DP, SLICE).astype(BF16)


def gateup_kernel(at_ref, x_ref, wg_ref, wu_ref, after_ref, keep_ref, send_ref):
    core = at_ref[1]
    for e in range(2):
        lhs = x_ref[:, 16 * e : 16 * e + 32, :].reshape(N_DP * 32, SLICE)
        halves = []
        for w_ref in (wg_ref, wu_ref):
            full = jnp.dot(lhs, w_ref[e], preferred_element_type=F32)
            full = full.reshape(N_DP, 32, 256)[:, 8 * e : 8 * e + 24, :].reshape(HALF, 256)
            halves.append((full[:, :128], full[:, 128:]))
        (g0, g1), (u0, u1) = halves
        first = core == 0
        keep_ref[0, e, :, :128] = jnp.where(first, g0, g1).astype(BF16)
        keep_ref[0, e, :, 128:] = jnp.where(first, u0, u1).astype(BF16)
        send_ref[0, e, :, :128] = jnp.where(first, g1, g0).astype(BF16)
        send_ref[0, e, :, 128:] = jnp.where(first, u1, u0).astype(BF16)


def gate_up(at, x, w_gate, w_up, after):
    wspec = pl.BlockSpec((2, SLICE, 256), lambda r, a: (0, 0, (a[0] + r) % 4))
    ospec = pl.BlockSpec((1, 2, HALF, 256), lambda r, a: (r, 0, 0, 0))
    shape = jax.ShapeDtypeStruct((4, 2, HALF, 256), BF16)
    return pl.pallas_call(
        gateup_kernel,
        grid_spec=pltpu.PrefetchScalarGridSpec(
            num_scalar_prefetch=1,
            grid=(4,),
            in_specs=[
                pl.BlockSpec((N_DP, PER_DP, SLICE), lambda r, a: (0, 0, 0)),
                wspec,
                wspec,
                ANY,
            ],
            out_specs=[ospec, ospec],
        ),
        out_shape=[shape, shape],
        compiler_params=PARAMS,
        cost_estimate=cost(4e9, 12e6),
        name="gate_up",
    )(at, x, w_gate, w_up, after)


def down_kernel(at_ref, *refs):
    acts = refs[:8]
    w_ref = refs[8]
    out_ref = refs[9]
    x = at_ref[0]
    first = at_ref[1] == 0
    results = []
    for e in range(2):
        total = jnp.zeros((HALF, SLICE), F32)
        for n, shift in enumerate((0, 3, 1, 2)):
            own = acts[n][e]
            other = acts[4 + n][e]
            low = jnp.where(first, own, other)
            high = jnp.where(first, other, own)
            lhs = jnp.concatenate([low, high], axis=1)
            chip = (x + shift) & 3
            rhs = w_ref[e, pl.ds(pl.multiple_of(chip * 256, 256), 256), :]
            total = total + jnp.dot(lhs, rhs, preferred_element_type=F32)
        results.append(total.reshape(N_DP, PER_DP // 2, SLICE))
    out_ref[...] = jnp.concatenate(results, axis=1).astype(BF16)


def down(at, acts, w_down):
    return pl.pallas_call(
        down_kernel,
        in_specs=[pl.BlockSpec(memory_space=pltpu.SMEM)] + [VMEM] * 9,
        out_specs=VMEM,
        out_shape=jax.ShapeDtypeStruct((N_DP, PER_DP, SLICE), BF16),
        compiler_params=PARAMS,
        cost_estimate=cost(2e9, 8e6),
        name="down",
    )(at, *acts, w_down)


def combine_kernel(s, at_ref, r_ref, ret_ref, wl_ref, own_ref, other_ref, all_ref):
    hid, _, _, gm, place = unpack(r_ref, s)
    weights = place(gm)
    high = weights.astype(BF16)
    low = (weights - high.astype(F32)).astype(BF16)
    ret = ret_ref[...].reshape(SLOTS, SLICE)
    dims = (((0,), (0,)), ((), ()))
    mixed = lax.dot_general(high, ret, dims, preferred_element_type=F32)
    mixed = mixed + lax.dot_general(low, ret, dims, preferred_element_type=F32)
    resid = hid + mixed
    square = jnp.sum(resid * resid, axis=-1, keepdims=True)
    kv = lax.dot_general(
        resid.astype(BF16), wl_ref[...], (((1,), (1,)), ((), ())), preferred_element_type=F32
    )
    all_ref[:, :, :KV] = kv.reshape(N_EP, ROWS, KV)
    all_ref[:, :, KEYW:KVW] = jnp.broadcast_to(square, (N_EP * ROWS, KVW - KEYW)).reshape(
        N_EP, ROWS, KVW - KEYW
    )
    all_ref[:, :, KV:KEYW] = jnp.zeros((N_EP, ROWS, KEYW - KV), F32)
    all_ref[:, :, KVW:] = mixed.reshape(N_EP, ROWS, SLICE)
    for r in range(4):
        base = 2 * ((at_ref[0] - r) & 3)
        own_ref[r] = all_ref[base + at_ref[1]]
        other_ref[r] = all_ref[base + 1 - at_ref[1]]


def fold_kernel(own_ref, got_ref, *out_refs):
    for r, out_ref in enumerate(out_refs):
        out_ref[:, :KVW] = own_ref[r, :, :KVW] + got_ref[r, :, :KVW]
        out_ref[:, KVW : KVW + SLICE] = own_ref[r, :, KVW:]
        out_ref[:, KVW + SLICE :] = got_ref[r, :, KVW:]


def key_kernel(at_ref, u0_ref, u1_ref, u2_ref, u3_ref, cos_ref, sin_ref, key_ref, block_ref, mixed_ref):
    parts = (u0_ref, u1_ref, u2_ref, u3_ref)
    kv = sum(u[:, :KVW] for u in parts)
    core = at_ref[1]
    for r, u in enumerate(parts):
        chip = (at_ref[0] + r) & 3
        for which, j in enumerate((2 * chip + core, 2 * chip + 1 - core)):
            lanes = pl.ds(pl.multiple_of(j * SLICE, SLICE), SLICE)
            cut = slice(KVW + which * SLICE, KVW + (which + 1) * SLICE)
            mixed_ref[:, lanes] = u[:, cut]
    raw = kv[:, :KEYW] * lax.rsqrt(kv[:, KEYW : KEYW + 1] * (1.0 / D) + EPS)
    latent = raw[:, :LAT]
    latent = latent * lax.rsqrt(jnp.mean(latent * latent, axis=-1, keepdims=True) + EPS)
    part = raw[:, LAT:]
    lane = lax.broadcasted_iota(jnp.int32, part.shape, 1)
    turned = jnp.where(lane < 32, -pltpu.roll(part, 96, 1), pltpu.roll(part, 32, 1))
    rotated = part * cos_ref[...] + turned * sin_ref[...]
    key = jnp.concatenate([latent, rotated], axis=1)
    key_ref[...] = key.astype(BF16).astype(F32)
    tiles = [key[:, 128 * n : 128 * n + 128] for n in range(5)] + [jnp.zeros((ROWS, 128), F32)]
    block_ref[...] = jnp.concatenate(tiles, axis=0).astype(BF16)


def old_attention(q, kt, count):
    scores = lax.dot_general(q, kt, (((0,), (0,)), ((), ())), preferred_element_type=F32) * SCALE
    lane = lax.broadcasted_iota(jnp.int32, scores.shape, 1)
    valid = lane < count
    scores = jnp.where(valid, scores, -1e30)
    top = jnp.max(scores, axis=1, keepdims=True)
    weights = jnp.where(valid, jnp.exp(scores - top), 0.0)
    total = jnp.sum(weights, axis=1, keepdims=True)
    out = lax.dot_general(
        weights.astype(BF16), kt[:LAT], (((1,), (1,)), ((), ())), preferred_element_type=F32
    )
    return out, top, total


def store_old(out_ref, stat_ref, parts):
    out, top, total = parts
    lane = lax.broadcasted_iota(jnp.int32, (128, 128), 1)
    out_ref[0] = out
    stat_ref[0] = jnp.where(lane == 0, top, total)


def old0_kernel(len_ref, q_ref, kt_ref, out_ref, stat_ref):
    count = len_ref[pl.program_id(0)]
    store_old(out_ref, stat_ref, old_attention(q_ref[0, 0], kt_ref[0], count))


def old1_kernel(tab_ref, q_ref, kt_ref, after_ref, out_ref, stat_ref):
    count = tab_ref[pl.program_id(0)]
    store_old(out_ref, stat_ref, old_attention(q_ref[0, 0], kt_ref[0], count))


OLD_SHAPE = [
    jax.ShapeDtypeStruct((ROWS, 128, LAT), F32),
    jax.ShapeDtypeStruct((ROWS, 128, 128), F32),
]
OLD_SPECS = [
    pl.BlockSpec((1, 128, LAT), lambda t, a: (t, 0, 0)),
    pl.BlockSpec((1, 128, 128), lambda t, a: (t, 0, 0)),
]


def old0(lens, qt, cache_t):
    return pl.pallas_call(
        old0_kernel,
        grid_spec=pltpu.PrefetchScalarGridSpec(
            num_scalar_prefetch=1,
            grid=(ROWS,),
            in_specs=[
                pl.BlockSpec((1, 1, KV, 128), lambda t, a: (0, t, 0, 0)),
                pl.BlockSpec((1, KV, 512), lambda t, a: (t, 0, 0)),
            ],
            out_specs=OLD_SPECS,
        ),
        out_shape=OLD_SHAPE,
        compiler_params=PARAMS,
        cost_estimate=cost(5e9, 8e6),
        name="old0",
    )(lens, qt, cache_t)


def old1(table, qt, cache_t, after):
    return pl.pallas_call(
        old1_kernel,
        grid_spec=pltpu.PrefetchScalarGridSpec(
            num_scalar_prefetch=1,
            grid=(ROWS,),
            in_specs=[
                pl.BlockSpec((1, 1, KV, 128), lambda t, a: (1, t, 0, 0)),
                pl.BlockSpec((1, KV, 512), lambda t, a: (a[8 + t], 0, 0)),
                ANY,
            ],
            out_specs=OLD_SPECS,
        ),
        out_shape=OLD_SHAPE,
        compiler_params=PARAMS,
        cost_estimate=cost(5e9, 8e6),
        name="old1",
    )(table, qt, cache_t, after)


def add_new(q, old, keys):
    out, top, total = old
    lane = lax.broadcasted_iota(jnp.int32, (128, ROWS), 1)
    sub = lax.broadcasted_iota(jnp.int32, (ROWS, LAT), 0)
    scores = []
    values = []
    for key, row in keys:
        both = lax.dot_general(
            q, key[:, :KV].astype(BF16), (((0,), (1,)), ((), ())), preferred_element_type=F32
        )
        scores.append(jnp.sum(jnp.where(lane == row, both, 0.0), axis=1, keepdims=True) * SCALE)
        values.append(jnp.sum(jnp.where(sub == row, key[:, :LAT], 0.0), axis=0, keepdims=True))
    peak = top
    for s in scores:
        peak = jnp.maximum(peak, s)
    shrink = jnp.exp(top - peak)
    out = out * shrink
    total = total * shrink
    for s, v in zip(scores, values):
        w = jnp.exp(s - peak)
        total = total + w
        out = out + w * v
    return (out / total).astype(BF16)


def merge_kernel(step, tab_ref, q_ref, old_ref, stat_ref, *refs):
    out_ref = refs[-1]
    t = pl.program_id(0)
    if step == 0:
        keys = [(refs[0][...], t)]
    else:
        keys = [(refs[0][...], tab_ref[8 + t]), (refs[1][...], t)]
    old = (old_ref[0], stat_ref[0, :, 0:1], stat_ref[0, :, 1:2])
    out_ref[0, 0] = add_new(q_ref[0, 0], old, keys)


def merge(step, table, qt, old, keys, buffer):
    in_specs = [
        pl.BlockSpec((1, 1, KV, 128), lambda t, a: (step, t, 0, 0)),
        pl.BlockSpec((1, 128, LAT), lambda t, a: (t, 0, 0)),
        pl.BlockSpec((1, 128, 128), lambda t, a: (t, 0, 0)),
    ] + [pl.BlockSpec((ROWS, KEYW), lambda t, a: (0, 0))] * len(keys)
    args = [table, qt, *old, *keys]
    alias = {}
    if buffer is not None:
        in_specs.append(ANY)
        alias = {len(args): 0}
        args.append(buffer)
    return pl.pallas_call(
        functools.partial(merge_kernel, step),
        grid_spec=pltpu.PrefetchScalarGridSpec(
            num_scalar_prefetch=1,
            grid=(ROWS,),
            in_specs=in_specs,
            out_specs=pl.BlockSpec((1, 1, 128, LAT), lambda t, a: (step, t, 0, 0)),
        ),
        out_shape=jax.ShapeDtypeStruct((2, ROWS, 128, LAT), BF16),
        input_output_aliases=alias,
        compiler_params=PARAMS,
        cost_estimate=cost(1e8, 5e6),
        name="merge%d" % step,
    )(*args)


def moved_kernel(tab_ref, q_ref, kv_ref, keys_ref, key1_ref, buffer_ref, out_ref, kt_ref):
    k = pl.program_id(0)
    slot = tab_ref[24 + k]
    for j in range(N_DP):
        f, l = j // 4, j % 4
        kt_ref[144 * f : 144 * f + 144, 128 * l : 128 * l + 128] = kv_ref[j]
    raw = keys_ref[...].astype(F32)
    where = tab_ref[16 + k]
    pick = lax.broadcasted_iota(jnp.int32, (N_DP, ROWS, 1), 0) * ROWS
    pick = pick + lax.broadcasted_iota(jnp.int32, (N_DP, ROWS, 1), 1)
    rows = []
    for n in range(5):
        tile = jnp.where(pick == where, raw[:, 8 * n : 8 * n + 8, :], 0.0)
        rows.append(jnp.sum(jnp.sum(tile, axis=0), axis=0, keepdims=True))
    first = jnp.broadcast_to(jnp.concatenate(rows, axis=1), (ROWS, KEYW))
    q = q_ref[0, 0]
    old = old_attention(q, kt_ref[...], tab_ref[slot])
    out_ref[0, 0] = add_new(q, old, [(first, 0), (key1_ref[...], slot)])


def moved_rows(table, qt, landed, key1, buffer):
    return pl.pallas_call(
        moved_kernel,
        grid_spec=pltpu.PrefetchScalarGridSpec(
            num_scalar_prefetch=1,
            grid=(2,),
            in_specs=[
                pl.BlockSpec((1, 1, KV, 128), lambda k, a: (1, a[24 + k], 0, 0)),
                pl.BlockSpec((N_DP, 144, 128), lambda k, a: (0, k, 0)),
                pl.BlockSpec((N_DP, 48, 128), lambda k, a: (0, 6, 0)),
                pl.BlockSpec((ROWS, KEYW), lambda k, a: (0, 0)),
                ANY,
            ],
            out_specs=pl.BlockSpec((1, 1, 128, LAT), lambda k, a: (1, a[24 + k], 0, 0)),
            scratch_shapes=[pltpu.VMEM((KV, 512), BF16)],
        ),
        out_shape=jax.ShapeDtypeStruct((2, ROWS, 128, LAT), BF16),
        input_output_aliases={5: 0},
        compiler_params=PARAMS,
        cost_estimate=cost(6e8, 3e6),
        name="moved_rows",
    )(table, qt, landed, landed, key1, buffer)


def run_copies(copies):
    for c in copies:
        c.start()
    for c in copies:
        c.wait()


def cut_kernel(leaving_ref, cache_ref, after_ref, out_ref, sem):
    copies = []
    for q in range(2):
        row = leaving_ref[q]
        for j in range(N_DP):
            f, l = j // 4, j % 4
            src = cache_ref.at[row, pl.ds(144 * f, 144), pl.ds(128 * l, 128)]
            copies.append(pltpu.make_async_copy(src, out_ref.at[j, q], sem.at[q * N_DP + j]))
    run_copies(copies)


def cut_pieces(leaving, cache_t, after):
    return pl.pallas_call(
        cut_kernel,
        in_specs=[pl.BlockSpec(memory_space=pltpu.SMEM), ANY, ANY],
        out_specs=ANY,
        out_shape=jax.ShapeDtypeStruct((N_DP, 2, 144, 128), BF16),
        scratch_shapes=[pltpu.SemaphoreType.DMA((2 * N_DP,))],
        compiler_params=PARAMS,
        cost_estimate=cost(1e6, 3e6),
        name="cut_pieces",
    )(leaving, cache_t, after)


def forward_kernel(idx_ref, src_ref, key_ref, out_ref, sem):
    copies = []
    for d in range(N_DP):
        for k in range(2):
            n = 2 * d + k
            dst = out_ref.at[d, pl.ds(144 * k, 144)]
            copies.append(pltpu.make_async_copy(src_ref.at[idx_ref[n]], dst, sem.at[n]))
        dst = out_ref.at[d, pl.ds(288, 48)]
        copies.append(pltpu.make_async_copy(key_ref, dst, sem.at[2 * N_DP + d]))
    run_copies(copies)


def forward(idx, pieces, key_block):
    return pl.pallas_call(
        forward_kernel,
        in_specs=[pl.BlockSpec(memory_space=pltpu.SMEM), ANY, ANY],
        out_specs=ANY,
        out_shape=jax.ShapeDtypeStruct((N_DP, 336, 128), BF16),
        scratch_shapes=[pltpu.SemaphoreType.DMA((3 * N_DP,))],
        compiler_params=PARAMS,
        cost_estimate=cost(1e6, 3e6),
        name="forward",
    )(idx, pieces, key_block)


SIB = [(i, i ^ 1) for i in range(8)]
XP = [(i, (i + 2) % 8) for i in range(8)]
XM = [(i, (i - 2) % 8) for i in range(8)]
X2 = [(i, (i + 4) % 8) for i in range(8)]


def hop(v, pairs):
    return lax.ppermute(v, "ep", pairs)


def pair_sum(keep, send):
    got = hop(send, SIB)
    parts = [(keep[r].astype(F32) + got[r].astype(F32)).astype(BF16) for r in (1, 2, 3)]
    return keep[0].astype(F32) + got[0].astype(F32), parts


def finish(at, own, parts, w_down):
    a1 = hop(parts[0], XP)
    a2 = hop(parts[1], X2)
    a3 = hop(parts[2], XM)
    total = own + a1.astype(F32) + a2.astype(F32) + a3.astype(F32)
    act = (jax.nn.silu(total[..., :128]) * total[..., 128:]).astype(BF16)
    b1 = hop(act, XP)
    b3 = hop(act, XM)
    b2 = hop(act, X2)
    ours = [act, b1, b3, b2]
    theirs = [hop(v, SIB) for v in ours]
    return down(at, ours + theirs, w_down)


def make_keys(s, at, gathered, result, latent_t, cosine, sine):
    returned = lax.all_to_all(result, "dp", split_axis=0, concat_axis=0, tiled=True)
    smem = pl.BlockSpec(memory_space=pltpu.SMEM)
    width = KVW + SLICE
    shape = jax.ShapeDtypeStruct((4, ROWS, width), F32)
    own, other = pl.pallas_call(
        functools.partial(combine_kernel, s),
        in_specs=[smem, VMEM, VMEM, VMEM],
        out_specs=[VMEM, VMEM],
        out_shape=[shape, shape],
        scratch_shapes=[pltpu.VMEM((N_EP, ROWS, width), F32)],
        compiler_params=PARAMS,
        cost_estimate=cost(4e8, 4e6),
        name="combine%d" % s,
    )(at, gathered, returned, latent_t)
    got = hop(other, SIB)
    shape = jax.ShapeDtypeStruct((ROWS, width + SLICE), F32)
    sums = pl.pallas_call(
        fold_kernel,
        in_specs=[VMEM, VMEM],
        out_specs=[VMEM] * 4,
        out_shape=[shape] * 4,
        compiler_params=PARAMS,
        name="fold%d" % s,
    )(own, got)
    parts = [sums[0], hop(sums[1], XM), hop(sums[2], X2), hop(sums[3], XP)]
    return pl.pallas_call(
        key_kernel,
        in_specs=[smem] + [VMEM] * 6,
        out_specs=[VMEM] * 3,
        out_shape=[
            jax.ShapeDtypeStruct((ROWS, KEYW), F32),
            jax.ShapeDtypeStruct((48, 128), BF16),
            jax.ShapeDtypeStruct((ROWS, D), F32),
        ],
        compiler_params=PARAMS,
        name="key%d" % s,
    )(at, *parts, cosine, sine)


def local(
    hidden,
    expert_ids,
    expert_gates,
    w_gate,
    w_up,
    w_down,
    w_latent,
    queries,
    cache,
    lengths,
    came_from,
):
    my_dp = lax.axis_index("dp")
    my_ep = lax.axis_index("ep")
    my_dev = my_dp * N_EP + my_ep
    at = jnp.stack([my_ep // 2, my_ep % 2]).astype(jnp.int32)
    qt = jnp.swapaxes(queries, 2, 3)
    cache_t = jnp.swapaxes(cache, 1, 2)
    latent_t = w_latent.T

    packed = pl.pallas_call(
        pack_kernel,
        in_specs=[VMEM] * 3,
        out_specs=VMEM,
        out_shape=jax.ShapeDtypeStruct((N_EP, 2 * ROWS, WIDE), BF16),
        compiler_params=PARAMS,
        name="pack",
    )(hidden, expert_ids, expert_gates)
    gathered = lax.all_to_all(packed, "ep", split_axis=0, concat_axis=0, tiled=True)
    out_shape = jax.ShapeDtypeStruct((N_DP, PER_DP, SLICE), BF16)
    sends = pl.pallas_call(
        dispatch_kernel,
        in_specs=[VMEM],
        out_specs=[VMEM, VMEM],
        out_shape=[out_shape, out_shape],
        compiler_params=PARAMS,
        name="dispatch",
    )(gathered)

    table = lax.dynamic_index_in_dim(
        came_from.reshape(N_DP, N_EP, ROWS), my_ep, 1, keepdims=False
    )
    src_dp = table // (N_EP * ROWS)
    src_row = table % ROWS
    src_flat = (src_dp * ROWS + src_row).reshape(N_DP * ROWS)
    flat = lax.iota(jnp.int32, N_DP * ROWS)
    hit = src_flat[:, None] == flat[None, :]
    crosses = (flat // ROWS)[:, None] != (flat // ROWS)[None, :]
    away = jnp.any(hit & crosses, axis=0).reshape(N_DP, ROWS).astype(jnp.int32)
    rows_before = lax.iota(jnp.int32, ROWS)[:, None] < lax.iota(jnp.int32, ROWS)[None, :]
    label = jnp.sum(away[:, :, None] * rows_before[None], axis=1)
    label_of = jnp.sum(jnp.where(hit, label.reshape(1, -1), 0), axis=1).reshape(N_DP, ROWS)
    arriving = (src_dp != lax.iota(jnp.int32, N_DP)[:, None]).astype(jnp.int32)
    turn = jnp.sum(arriving[:, :, None] * rows_before[None], axis=1)
    source = src_dp * 2 + label_of
    pick = (turn[:, :, None] == lax.iota(jnp.int32, 2)) & (arriving[:, :, None] == 1)
    forward_idx = jnp.sum(jnp.where(pick, source[:, :, None], 0), axis=1).reshape(2 * N_DP)
    my_away = lax.dynamic_index_in_dim(away, my_dp, 0, keepdims=False)
    my_label = lax.dynamic_index_in_dim(label, my_dp, 0, keepdims=False)
    leave = (my_label[:, None] == lax.iota(jnp.int32, 2)) & (my_away[:, None] == 1)
    leaving = jnp.sum(jnp.where(leave, lax.iota(jnp.int32, ROWS)[:, None], 0), axis=0)
    my_src = lax.dynamic_index_in_dim(table, my_dp, 0, keepdims=False)
    my_src_flat = lax.dynamic_index_in_dim(
        src_flat.reshape(N_DP, ROWS), my_dp, 0, keepdims=False
    )
    my_arriving = lax.dynamic_index_in_dim(arriving, my_dp, 0, keepdims=False)
    my_turn = lax.dynamic_index_in_dim(turn, my_dp, 0, keepdims=False)
    own_len = lax.dynamic_slice_in_dim(lengths, my_dev * ROWS, ROWS)
    second_len = jnp.take(lengths, my_src)
    order = (my_turn[:, None] == lax.iota(jnp.int32, 2)) & (my_arriving[:, None] == 1)
    arrival_slot = jnp.sum(jnp.where(order, lax.iota(jnp.int32, ROWS)[:, None], 0), axis=0)
    arrival_src = jnp.sum(jnp.where(order, my_src_flat[:, None], 0), axis=0)
    pad = jnp.zeros((6,), jnp.int32)
    old_table = jnp.concatenate(
        [
            second_len,
            jnp.where(my_arriving == 1, 0, my_src % ROWS),
            arrival_src,
            pad,
            arrival_slot,
            pad,
        ]
    ).astype(jnp.int32)

    first_old = old0(own_len, qt, cache_t)

    positions = jnp.stack([own_len, second_len + 1]).astype(F32)
    freq = 10000.0 ** (-2.0 * jnp.arange(32, dtype=F32) / 64)
    angle = positions[:, :, None] * jnp.tile(freq, 4)[None, None, :]
    keep = jnp.arange(128) < 64
    cosine = jnp.where(keep, jnp.cos(angle), 0.0)
    sine = jnp.where(keep, jnp.sin(angle), 0.0)

    arrived = [
        lax.all_to_all(sends[s], "dp", split_axis=0, concat_axis=0, tiled=True) for s in range(2)
    ]
    keep, send = gate_up(at, arrived[0], w_gate, w_up, first_old[1])
    own0, parts0 = pair_sum(keep, send)
    second_old = old1(old_table, qt, cache_t, parts0[0])
    keep, send = gate_up(at, arrived[1], w_gate, w_up, second_old[1])
    own1, parts1 = pair_sum(keep, send)
    pieces = cut_pieces(leaving.astype(jnp.int32), cache_t, arrived[1])
    spread = lax.all_to_all(pieces, "dp", split_axis=0, concat_axis=0, tiled=True)
    result0 = finish(at, own0, parts0, w_down)
    result1 = finish(at, own1, parts1, w_down)
    key0, block0, mixed0 = make_keys(0, at, gathered, result0, latent_t, cosine[0], sine[0])
    attended = merge(0, old_table, qt, first_old, [key0], None)
    onward = forward(forward_idx, spread.reshape(2 * N_DP, 144, 128), block0)
    key1, _, mixed1 = make_keys(1, at, gathered, result1, latent_t, cosine[1], sine[1])
    landed = lax.all_to_all(onward, "dp", split_axis=0, concat_axis=0, tiled=True)
    attended = merge(1, old_table, qt, second_old, [key0, key1], attended)
    attended = moved_rows(old_table, qt, landed, key1, attended)
    expert_out = jnp.stack([mixed0, mixed1]).astype(BF16)
    return (expert_out, attended)


def solution(mesh):
    in_specs = (
        P(None, ("dp", "ep"), None),
        P(None, ("dp", "ep"), None),
        P(None, ("dp", "ep"), None),
        P("dp", "ep", None),
        P("dp", "ep", None),
        P("dp", None, "ep"),
        P("ep", None),
        P(None, ("dp", "ep"), None, None),
        P(("dp", "ep"), None, None),
        P(),
        P(),
    )
    out_specs = (P(None, ("dp", "ep"), None), P(None, ("dp", "ep"), None, None))
    return jax.shard_map(local, mesh=mesh, in_specs=in_specs, out_specs=out_specs, check_vma=False)
```

```python
import functools

import jax
import jax.numpy as jnp
import numpy as np
from jax import lax
from jax.experimental import pallas as pl
from jax.experimental.pallas import tpu as pltpu
from jax.sharding import PartitionSpec as P

F32 = jnp.float32
BF16 = jnp.bfloat16
D = 7168
LAT = 512
KV = 576
FF = 1024
EXPERTS = 32
CAP = 3
N_DP = 16
N_EP = 8
SLICE = D // N_EP
META = 128
WIDE = SLICE + META
ROWS = 8
TOPK = 8
SLOTS = EXPERTS * CAP * N_EP
PER_DP = SLOTS // N_DP
HALF = SLOTS // 2
KVW = 768
KEYW = 640
SCALE = 192.0 ** (-0.5)
EPS = 1e-06
VMEM = pl.BlockSpec(memory_space=pltpu.VMEM)
ANY = pl.BlockSpec(memory_space=pl.ANY)
PARAMS = pltpu.CompilerParams(vmem_limit_bytes=48 * 1024 * 1024)


def cost(flops, nbytes):
    return pl.CostEstimate(flops=int(flops), bytes_accessed=int(nbytes), transcendentals=0)


def split3(v):
    hi = v.astype(BF16).astype(F32)
    mid = (v - hi).astype(BF16).astype(F32)
    lo = (v - hi - mid).astype(BF16).astype(F32)
    return hi, mid, lo


def pack_kernel(hidden_ref, ids_ref, gates_ref, out_ref):
    lane = lax.broadcasted_iota(jnp.int32, (ROWS, META), 1)
    rows = []
    metas = []
    for s in range(2):
        h = hidden_ref[s].astype(F32)
        scale = lax.rsqrt(jnp.mean(h * h, axis=-1, keepdims=True) + EPS)
        ids = ids_ref[s].astype(F32)
        parts = split3(gates_ref[s])
        meta = jnp.zeros((ROWS, META), F32)
        for k in range(TOPK):
            meta = jnp.where(lane == k, ids[:, k : k + 1], meta)
            for n, part in enumerate(parts):
                meta = jnp.where(lane == 8 + 8 * n + k, part[:, k : k + 1], meta)
        for n, part in enumerate(split3(scale)):
            meta = jnp.where(lane == 32 + n, part, meta)
        rows.append(h)
        metas.append(meta)
    meta = jnp.concatenate(metas, axis=0).astype(BF16)
    for j in range(N_EP):
        cut = slice(j * SLICE, (j + 1) * SLICE)
        both = jnp.concatenate([rows[0][:, cut], rows[1][:, cut]], axis=0)
        out_ref[j, :, :SLICE] = both.astype(BF16)
        out_ref[j, :, SLICE:] = meta


def unpack(r_ref, s):
    rows = r_ref[...].astype(F32)[:, 8 * s : 8 * s + 8, :].reshape(N_EP * ROWS, WIDE)
    n = N_EP * ROWS
    hid = rows[:, :SLICE]
    meta = rows[:, SLICE:]
    mt = meta.T
    ids = mt[0:8]
    gates = mt[8:16] + mt[16:24] + mt[24:32]
    scale = meta[:, 32:33] + meta[:, 33:34] + meta[:, 34:35]
    expert = lax.broadcasted_iota(jnp.int32, (EXPERTS, n), 0).astype(F32)
    onehot = jnp.zeros((EXPERTS, n), F32)
    gm = jnp.zeros((EXPERTS, n), F32)
    for k in range(TOPK):
        eq = expert == ids[k : k + 1]
        onehot = jnp.where(eq, 1.0, onehot)
        gm = jnp.where(eq, gates[k : k + 1], gm)
    p = lax.broadcasted_iota(jnp.int32, (n, n), 0)
    q = lax.broadcasted_iota(jnp.int32, (n, n), 1)
    earlier = jnp.where(((p >> 3) == (q >> 3)) & (p < q), 1.0, 0.0).astype(BF16)
    rank = jnp.dot(onehot.astype(BF16), earlier, preferred_element_type=F32)
    b = lax.broadcasted_iota(jnp.int32, (N_EP, n), 0)
    qq = lax.broadcasted_iota(jnp.int32, (N_EP, n), 1)
    block = jnp.where((qq >> 3) == b, 1.0, 0.0)

    def place(values):
        pieces = []
        for r in range(CAP):
            picked = jnp.where((rank == float(r)) & (onehot > 0.0), values, 0.0)
            pieces.append((picked[:, None, :] * block[None, :, :])[:, None])
        return jnp.concatenate(pieces, axis=1).reshape(SLOTS, n)

    return hid, scale, onehot, gm, place


def dispatch_kernel(r_ref, out0_ref, out1_ref):
    for s, out_ref in enumerate((out0_ref, out1_ref)):
        hid, scale, onehot, _, place = unpack(r_ref, s)
        normed = (hid * scale).astype(BF16)
        table = place(onehot).astype(BF16)
        out = jnp.dot(table, normed, preferred_element_type=F32)
        out_ref[...] = out.reshape(N_DP, PER_DP, SLICE).astype(BF16)


def total(values, axis):
    return jnp.sum(values, axis=axis, keepdims=True)


def table_kernel(me_ref, from_ref, len_ref, freq_ref, tab_ref, cos_ref, sin_ref, hold_ref):
    n = N_DP * ROWS
    my_dp, my_ep = me_ref[0], me_ref[1]
    sub = lax.broadcasted_iota(jnp.int32, (n, n), 0)
    lane = lax.broadcasted_iota(jnp.int32, (n, n), 1)
    lane64 = lax.broadcasted_iota(jnp.int32, (n, 64), 1)
    sub64 = lax.broadcasted_iota(jnp.int32, (n, 64), 0)
    wanted = lane64 == my_ep * ROWS + (sub64 & 7)

    def column(ref):
        wide = jnp.broadcast_to(ref[...][:, None, :], (N_DP, ROWS, 64)).reshape(n, 64)
        return total(jnp.where(wanted, wide, 0), 1)

    def as_row(col):
        return total(jnp.where(sub == lane, col, 0), 0)

    came = column(from_ref)
    lens = column(len_ref)
    src_dp = came >> 6
    src = src_dp * ROWS + (came & 7)
    home = lax.broadcasted_iota(jnp.int32, (n, 1), 0)
    arriving = src_dp != (home >> 3)
    arriving_row = as_row(arriving.astype(jnp.int32))
    hit = src == lane
    away_row = total(jnp.where(hit & arriving, 1, 0), 0)
    label = total(jnp.where(((src >> 3) == (lane >> 3)) & (lane < src), away_row, 0), 1)
    turn = total(jnp.where(((sub >> 3) == (lane >> 3)) & (lane < sub), arriving_row, 0), 1)
    second = total(jnp.where(hit, as_row(lens), 0), 1)
    mine = sub == my_dp * ROWS + lane
    here = ((sub >> 3) == my_dp) & arriving & (turn == lane)
    onward = ((sub >> 3) == (lane >> 1)) & arriving & (turn == (lane & 1)) & (lane < 2 * N_DP)
    gone = ((src >> 3) == my_dp) & arriving & (label == lane)
    lane_row = lax.broadcasted_iota(jnp.int32, (1, n), 1)
    spot = jnp.where(lane_row == 0, my_ep >> 1, jnp.where(lane_row == 1, my_ep & 1, 0))
    rows = [
        total(jnp.where(mine, second, 0), 0),
        total(jnp.where(mine & ~arriving, src & 7, 0), 0),
        total(jnp.where(here, src, 0), 0),
        total(jnp.where(here, home & 7, 0), 0),
        total(jnp.where(onward, src_dp * 2 + label, 0), 0),
        total(jnp.where(gone, src & 7, 0), 0),
        total(jnp.where(mine, lens, 0), 0),
        spot,
    ]
    tab_ref[...] = jnp.concatenate(rows, axis=0)
    hold_ref[0] = lens.astype(F32)
    hold_ref[1] = (second + 1).astype(F32)
    live = lax.broadcasted_iota(jnp.int32, (ROWS, 128), 1) < 64
    for s in range(2):
        angle = hold_ref[s, pl.ds(pl.multiple_of(my_dp * ROWS, ROWS), ROWS), :] * freq_ref[...]
        cos_ref[s] = jnp.where(live, jnp.cos(angle), 0.0)
        sin_ref[s] = jnp.where(live, jnp.sin(angle), 0.0)


def make_table(me, came_from, lengths):
    freq = jnp.asarray(np.tile(10000.0 ** (-2.0 * np.arange(32) / 64), 4)[None], F32)
    wave = jax.ShapeDtypeStruct((2, ROWS, 128), F32)
    return pl.pallas_call(
        table_kernel,
        in_specs=[pl.BlockSpec(memory_space=pltpu.SMEM)] + [VMEM] * 3,
        out_specs=[VMEM] * 3,
        out_shape=[jax.ShapeDtypeStruct((8, 128), jnp.int32), wave, wave],
        scratch_shapes=[pltpu.VMEM((2, N_DP * ROWS, 1), F32)],
        compiler_params=PARAMS,
        name="table",
    )(me, came_from.reshape(N_DP, 64), lengths.reshape(N_DP, 64), freq)


def gateup_kernel(at_ref, x_ref, wg_ref, wu_ref, after_ref, also_ref, keep_ref, send_ref):
    core = at_ref[1]
    for e in range(2):
        lhs = x_ref[:, 16 * e : 16 * e + 32, :].reshape(N_DP * 32, SLICE)
        halves = []
        for w_ref in (wg_ref, wu_ref):
            full = jnp.dot(lhs, w_ref[e], preferred_element_type=F32)
            full = full.reshape(N_DP, 32, 256)[:, 8 * e : 8 * e + 24, :].reshape(HALF, 256)
            halves.append((full[:, :128], full[:, 128:]))
        (g0, g1), (u0, u1) = halves
        first = core == 0
        keep_ref[0, e, :, :128] = jnp.where(first, g0, g1).astype(BF16)
        keep_ref[0, e, :, 128:] = jnp.where(first, u0, u1).astype(BF16)
        send_ref[0, e, :, :128] = jnp.where(first, g1, g0).astype(BF16)
        send_ref[0, e, :, 128:] = jnp.where(first, u1, u0).astype(BF16)


def gate_up(at, x, w_gate, w_up, after, also):
    wspec = pl.BlockSpec((2, SLICE, 256), lambda r, a: (0, 0, (a[0] + r) % 4))
    ospec = pl.BlockSpec((1, 2, HALF, 256), lambda r, a: (r, 0, 0, 0))
    shape = jax.ShapeDtypeStruct((4, 2, HALF, 256), BF16)
    return pl.pallas_call(
        gateup_kernel,
        grid_spec=pltpu.PrefetchScalarGridSpec(
            num_scalar_prefetch=1,
            grid=(4,),
            in_specs=[
                pl.BlockSpec((N_DP, PER_DP, SLICE), lambda r, a: (0, 0, 0)),
                wspec,
                wspec,
                ANY,
                ANY,
            ],
            out_specs=[ospec, ospec],
        ),
        out_shape=[shape, shape],
        compiler_params=PARAMS,
        cost_estimate=cost(4e9, 12e6),
        name="gate_up",
    )(at, x, w_gate, w_up, after, also)


def down_kernel(at_ref, *refs):
    acts = refs[:8]
    w_ref = refs[8]
    out_ref = refs[-1]
    x = at_ref[0]
    first = at_ref[1] == 0
    results = []
    for e in range(2):
        total = jnp.zeros((HALF, SLICE), F32)
        for n, shift in enumerate((0, 3, 1, 2)):
            own = acts[n][e]
            other = acts[4 + n][e]
            low = jnp.where(first, own, other)
            high = jnp.where(first, other, own)
            lhs = jnp.concatenate([low, high], axis=1)
            chip = (x + shift) & 3
            rhs = w_ref[e, pl.ds(pl.multiple_of(chip * 256, 256), 256), :]
            total = total + jnp.dot(lhs, rhs, preferred_element_type=F32)
        results.append(total.reshape(N_DP, PER_DP // 2, SLICE))
    out_ref[...] = jnp.concatenate(results, axis=1).astype(BF16)


def down(at, acts, w_down, after):
    return pl.pallas_call(
        down_kernel,
        in_specs=[pl.BlockSpec(memory_space=pltpu.SMEM)] + [VMEM] * 9 + [ANY],
        out_specs=VMEM,
        out_shape=jax.ShapeDtypeStruct((N_DP, PER_DP, SLICE), BF16),
        compiler_params=PARAMS,
        cost_estimate=cost(2e9, 8e6),
        name="down",
    )(at, *acts, w_down, after)


def combine_kernel(s, at_ref, r_ref, ret_ref, wl_ref, after_ref, own_ref, other_ref, all_ref):
    hid, _, _, gm, place = unpack(r_ref, s)
    weights = place(gm)
    high = weights.astype(BF16)
    low = (weights - high.astype(F32)).astype(BF16)
    ret = ret_ref[...].reshape(SLOTS, SLICE)
    dims = (((0,), (0,)), ((), ()))
    mixed = lax.dot_general(high, ret, dims, preferred_element_type=F32)
    mixed = mixed + lax.dot_general(low, ret, dims, preferred_element_type=F32)
    resid = hid + mixed
    square = jnp.sum(resid * resid, axis=-1, keepdims=True)
    kv = lax.dot_general(
        resid.astype(BF16), wl_ref[...], (((1,), (1,)), ((), ())), preferred_element_type=F32
    )
    all_ref[:, :, :KV] = kv.reshape(N_EP, ROWS, KV)
    all_ref[:, :, KEYW:KVW] = jnp.broadcast_to(square, (N_EP * ROWS, KVW - KEYW)).reshape(
        N_EP, ROWS, KVW - KEYW
    )
    all_ref[:, :, KV:KEYW] = jnp.zeros((N_EP, ROWS, KEYW - KV), F32)
    all_ref[:, :, KVW:] = mixed.reshape(N_EP, ROWS, SLICE)
    for r in range(4):
        base = 2 * ((at_ref[0] - r) & 3)
        own_ref[r] = all_ref[base + at_ref[1]]
        other_ref[r] = all_ref[base + 1 - at_ref[1]]


def fold_kernel(own_ref, got_ref, *out_refs):
    for r, out_ref in enumerate(out_refs):
        out_ref[:, :KVW] = own_ref[r, :, :KVW] + got_ref[r, :, :KVW]
        out_ref[:, KVW : KVW + SLICE] = own_ref[r, :, KVW:]
        out_ref[:, KVW + SLICE :] = got_ref[r, :, KVW:]


def key_kernel(at_ref, u0_ref, u1_ref, u2_ref, u3_ref, cos_ref, sin_ref, key_ref, block_ref, mixed_ref):
    parts = (u0_ref, u1_ref, u2_ref, u3_ref)
    kv = sum(u[:, :KVW] for u in parts)
    core = at_ref[1]
    for r, u in enumerate(parts):
        chip = (at_ref[0] + r) & 3
        for which, j in enumerate((2 * chip + core, 2 * chip + 1 - core)):
            lanes = pl.ds(pl.multiple_of(j * SLICE, SLICE), SLICE)
            cut = slice(KVW + which * SLICE, KVW + (which + 1) * SLICE)
            mixed_ref[:, lanes] = u[:, cut]
    raw = kv[:, :KEYW] * lax.rsqrt(kv[:, KEYW : KEYW + 1] * (1.0 / D) + EPS)
    latent = raw[:, :LAT]
    latent = latent * lax.rsqrt(jnp.mean(latent * latent, axis=-1, keepdims=True) + EPS)
    part = raw[:, LAT:]
    lane = lax.broadcasted_iota(jnp.int32, part.shape, 1)
    turned = jnp.where(lane < 32, -pltpu.roll(part, 96, 1), pltpu.roll(part, 32, 1))
    rotated = part * cos_ref[...] + turned * sin_ref[...]
    key = jnp.concatenate([latent, rotated], axis=1)
    key_ref[...] = key.astype(BF16).astype(F32)
    tiles = [key[:, 128 * n : 128 * n + 128] for n in range(5)] + [jnp.zeros((ROWS, 128), F32)]
    block_ref[...] = jnp.concatenate(tiles, axis=0).astype(BF16)


def old_attention(q, kt, count):
    scores = lax.dot_general(q, kt, (((0,), (0,)), ((), ())), preferred_element_type=F32) * SCALE
    lane = lax.broadcasted_iota(jnp.int32, scores.shape, 1)
    valid = lane < count
    scores = jnp.where(valid, scores, -1e30)
    top = jnp.max(scores, axis=1, keepdims=True)
    weights = jnp.where(valid, jnp.exp(scores - top), 0.0)
    total = jnp.sum(weights, axis=1, keepdims=True)
    out = lax.dot_general(
        weights.astype(BF16), kt[:LAT], (((1,), (1,)), ((), ())), preferred_element_type=F32
    )
    return out, top, total


def store_old(out_ref, stat_ref, parts):
    out, top, total = parts
    lane = lax.broadcasted_iota(jnp.int32, (128, 128), 1)
    out_ref[0] = out
    stat_ref[0] = jnp.where(lane == 0, top, total)


def old0_kernel(len_ref, q_ref, kt_ref, out_ref, stat_ref):
    count = len_ref[6, pl.program_id(0)]
    store_old(out_ref, stat_ref, old_attention(q_ref[0, 0], kt_ref[0], count))


def old1_kernel(tab_ref, q_ref, kt_ref, after_ref, out_ref, stat_ref):
    count = tab_ref[0, pl.program_id(0)]
    store_old(out_ref, stat_ref, old_attention(q_ref[0, 0], kt_ref[0], count))


OLD_SHAPE = [
    jax.ShapeDtypeStruct((ROWS, 128, LAT), F32),
    jax.ShapeDtypeStruct((ROWS, 128, 128), F32),
]
OLD_SPECS = [
    pl.BlockSpec((1, 128, LAT), lambda t, a: (t, 0, 0)),
    pl.BlockSpec((1, 128, 128), lambda t, a: (t, 0, 0)),
]


def old0(lens, qt, cache_t):
    return pl.pallas_call(
        old0_kernel,
        grid_spec=pltpu.PrefetchScalarGridSpec(
            num_scalar_prefetch=1,
            grid=(ROWS,),
            in_specs=[
                pl.BlockSpec((1, 1, KV, 128), lambda t, a: (0, t, 0, 0)),
                pl.BlockSpec((1, KV, 512), lambda t, a: (t, 0, 0)),
            ],
            out_specs=OLD_SPECS,
        ),
        out_shape=OLD_SHAPE,
        compiler_params=PARAMS,
        cost_estimate=cost(5e9, 8e6),
        name="old0",
    )(lens, qt, cache_t)


def old1(table, qt, cache_t, after):
    return pl.pallas_call(
        old1_kernel,
        grid_spec=pltpu.PrefetchScalarGridSpec(
            num_scalar_prefetch=1,
            grid=(ROWS,),
            in_specs=[
                pl.BlockSpec((1, 1, KV, 128), lambda t, a: (1, t, 0, 0)),
                pl.BlockSpec((1, KV, 512), lambda t, a: (a[1, t], 0, 0)),
                ANY,
            ],
            out_specs=OLD_SPECS,
        ),
        out_shape=OLD_SHAPE,
        compiler_params=PARAMS,
        cost_estimate=cost(5e9, 8e6),
        name="old1",
    )(table, qt, cache_t, after)


def add_new(q, old, keys):
    out, top, total = old
    lane = lax.broadcasted_iota(jnp.int32, (128, ROWS), 1)
    sub = lax.broadcasted_iota(jnp.int32, (ROWS, LAT), 0)
    scores = []
    values = []
    for key, row in keys:
        both = jnp.dot(key[:, :KV].astype(BF16), q, preferred_element_type=F32).T
        scores.append(jnp.sum(jnp.where(lane == row, both, 0.0), axis=1, keepdims=True) * SCALE)
        values.append(jnp.sum(jnp.where(sub == row, key[:, :LAT], 0.0), axis=0, keepdims=True))
    peak = top
    for s in scores:
        peak = jnp.maximum(peak, s)
    shrink = jnp.exp(top - peak)
    out = out * shrink
    total = total * shrink
    for s, v in zip(scores, values):
        w = jnp.exp(s - peak)
        total = total + w
        out = out + w * v
    return (out / total).astype(BF16)


def merge_kernel(step, tab_ref, q_ref, old_ref, stat_ref, *refs):
    out_ref = refs[-1]
    t = pl.program_id(0)
    if step == 0:
        keys = [(refs[0][...], t)]
    else:
        keys = [(refs[0][...], tab_ref[1, t]), (refs[1][...], t)]
    old = (old_ref[0], stat_ref[0, :, 0:1], stat_ref[0, :, 1:2])
    out_ref[0, 0] = add_new(q_ref[0, 0], old, keys)


def merge(step, table, qt, old, keys, buffer):
    in_specs = [
        pl.BlockSpec((1, 1, KV, 128), lambda t, a: (step, t, 0, 0)),
        pl.BlockSpec((1, 128, LAT), lambda t, a: (t, 0, 0)),
        pl.BlockSpec((1, 128, 128), lambda t, a: (t, 0, 0)),
    ] + [pl.BlockSpec((ROWS, KEYW), lambda t, a: (0, 0))] * len(keys)
    args = [table, qt, *old, *keys]
    alias = {}
    if buffer is not None:
        in_specs.append(ANY)
        alias = {len(args): 0}
        args.append(buffer)
    return pl.pallas_call(
        functools.partial(merge_kernel, step),
        grid_spec=pltpu.PrefetchScalarGridSpec(
            num_scalar_prefetch=1,
            grid=(ROWS,),
            in_specs=in_specs,
            out_specs=pl.BlockSpec((1, 1, 128, LAT), lambda t, a: (step, t, 0, 0)),
        ),
        out_shape=jax.ShapeDtypeStruct((2, ROWS, 128, LAT), BF16),
        input_output_aliases=alias,
        compiler_params=PARAMS,
        cost_estimate=cost(1e8, 5e6),
        name="merge%d" % step,
    )(*args)


def moved_kernel(tab_ref, q_ref, kv_ref, keys_ref, key1_ref, buffer_ref, out_ref, kt_ref):
    k = pl.program_id(0)
    slot = tab_ref[3, k]
    for j in range(N_DP):
        f, l = j // 4, j % 4
        kt_ref[144 * f : 144 * f + 144, 128 * l : 128 * l + 128] = kv_ref[j]
    raw = keys_ref[...].astype(F32)
    where = tab_ref[2, k]
    pick = lax.broadcasted_iota(jnp.int32, (N_DP, ROWS, 1), 0) * ROWS
    pick = pick + lax.broadcasted_iota(jnp.int32, (N_DP, ROWS, 1), 1)
    rows = []
    for n in range(5):
        tile = jnp.where(pick == where, raw[:, 8 * n : 8 * n + 8, :], 0.0)
        rows.append(jnp.sum(jnp.sum(tile, axis=0), axis=0, keepdims=True))
    first = jnp.broadcast_to(jnp.concatenate(rows, axis=1), (ROWS, KEYW))
    q = q_ref[0, 0]
    old = old_attention(q, kt_ref[...], tab_ref[0, slot])
    out_ref[0, 0] = add_new(q, old, [(first, 0), (key1_ref[...], slot)])


def moved_rows(table, qt, landed, key1, buffer):
    return pl.pallas_call(
        moved_kernel,
        grid_spec=pltpu.PrefetchScalarGridSpec(
            num_scalar_prefetch=1,
            grid=(2,),
            in_specs=[
                pl.BlockSpec((1, 1, KV, 128), lambda k, a: (1, a[3, k], 0, 0)),
                pl.BlockSpec((N_DP, 144, 128), lambda k, a: (0, k, 0)),
                pl.BlockSpec((N_DP, 48, 128), lambda k, a: (0, 6, 0)),
                pl.BlockSpec((ROWS, KEYW), lambda k, a: (0, 0)),
                ANY,
            ],
            out_specs=pl.BlockSpec((1, 1, 128, LAT), lambda k, a: (1, a[3, k], 0, 0)),
            scratch_shapes=[pltpu.VMEM((KV, 512), BF16)],
        ),
        out_shape=jax.ShapeDtypeStruct((2, ROWS, 128, LAT), BF16),
        input_output_aliases={5: 0},
        compiler_params=PARAMS,
        cost_estimate=cost(6e8, 3e6),
        name="moved_rows",
    )(table, qt, landed, landed, key1, buffer)


def run_copies(copies):
    for c in copies:
        c.start()
    for c in copies:
        c.wait()


def cut_kernel(leaving_ref, cache_ref, after_ref, out_ref, sem):
    copies = []
    for q in range(2):
        row = leaving_ref[5, q]
        for j in range(N_DP):
            f, l = j // 4, j % 4
            src = cache_ref.at[row, pl.ds(144 * f, 144), pl.ds(128 * l, 128)]
            copies.append(pltpu.make_async_copy(src, out_ref.at[j, q], sem.at[q * N_DP + j]))
    run_copies(copies)


def cut_pieces(leaving, cache_t, after):
    return pl.pallas_call(
        cut_kernel,
        in_specs=[pl.BlockSpec(memory_space=pltpu.SMEM), ANY, ANY],
        out_specs=VMEM,
        out_shape=jax.ShapeDtypeStruct((N_DP, 2, 144, 128), BF16),
        scratch_shapes=[pltpu.SemaphoreType.DMA((2 * N_DP,))],
        compiler_params=PARAMS,
        cost_estimate=cost(1e6, 3e6),
        name="cut_pieces",
    )(leaving, cache_t, after)


def forward_kernel(idx_ref, src_ref, key_ref, out_ref, sem):
    copies = []
    for d in range(N_DP):
        for k in range(2):
            n = 2 * d + k
            dst = out_ref.at[d, pl.ds(144 * k, 144)]
            copies.append(pltpu.make_async_copy(src_ref.at[idx_ref[4, n]], dst, sem.at[n]))
        dst = out_ref.at[d, pl.ds(288, 48)]
        copies.append(pltpu.make_async_copy(key_ref, dst, sem.at[2 * N_DP + d]))
    run_copies(copies)


def forward(idx, pieces, key_block):
    return pl.pallas_call(
        forward_kernel,
        in_specs=[pl.BlockSpec(memory_space=pltpu.SMEM), VMEM, VMEM],
        out_specs=VMEM,
        out_shape=jax.ShapeDtypeStruct((N_DP, 336, 128), BF16),
        scratch_shapes=[pltpu.SemaphoreType.DMA((3 * N_DP,))],
        compiler_params=PARAMS,
        cost_estimate=cost(1e6, 3e6),
        name="forward",
    )(idx, pieces, key_block)


SIB = [(i, i ^ 1) for i in range(8)]
XP = [(i, (i + 2) % 8) for i in range(8)]
XM = [(i, (i - 2) % 8) for i in range(8)]
X2 = [(i, (i + 4) % 8) for i in range(8)]


def to_dp(v):
    return lax.all_to_all(v, "dp", split_axis=0, concat_axis=0, tiled=True)


def hop(v, pairs):
    return lax.ppermute(v, "ep", pairs)


def pair_sum(keep, send):
    got = hop(send, SIB)
    parts = [(keep[r].astype(F32) + got[r].astype(F32)).astype(BF16) for r in (1, 2, 3)]
    return keep[0].astype(F32) + got[0].astype(F32), parts


def activate(own, parts):
    a1 = hop(parts[0], XP)
    a2 = hop(parts[1], X2)
    a3 = hop(parts[2], XM)
    total = own + a1.astype(F32) + a2.astype(F32) + a3.astype(F32)
    return (jax.nn.silu(total[..., :128]) * total[..., 128:]).astype(BF16)


def finish(at, act, w_down, after):
    b1 = hop(act, XP)
    b3 = hop(act, XM)
    b2 = hop(act, X2)
    ours = [act, b1, b3, b2]
    theirs = [hop(v, SIB) for v in ours]
    return down(at, ours + theirs, w_down, after)


def make_keys(s, at, gathered, returned, latent_t, cosine, sine, after):
    smem = pl.BlockSpec(memory_space=pltpu.SMEM)
    width = KVW + SLICE
    shape = jax.ShapeDtypeStruct((4, ROWS, width), F32)
    own, other = pl.pallas_call(
        functools.partial(combine_kernel, s),
        in_specs=[smem, VMEM, VMEM, VMEM, ANY],
        out_specs=[VMEM, VMEM],
        out_shape=[shape, shape],
        scratch_shapes=[pltpu.VMEM((N_EP, ROWS, width), F32)],
        compiler_params=PARAMS,
        cost_estimate=cost(4e8, 4e6),
        name="combine%d" % s,
    )(at, gathered, returned, latent_t, after)
    got = hop(other, SIB)
    shape = jax.ShapeDtypeStruct((ROWS, width + SLICE), F32)
    sums = pl.pallas_call(
        fold_kernel,
        in_specs=[VMEM, VMEM],
        out_specs=[VMEM] * 4,
        out_shape=[shape] * 4,
        compiler_params=PARAMS,
        name="fold%d" % s,
    )(own, got)
    parts = [sums[0], hop(sums[1], XM), hop(sums[2], X2), hop(sums[3], XP)]
    return pl.pallas_call(
        key_kernel,
        in_specs=[smem] + [VMEM] * 6,
        out_specs=[VMEM] * 3,
        out_shape=[
            jax.ShapeDtypeStruct((ROWS, KEYW), F32),
            jax.ShapeDtypeStruct((48, 128), BF16),
            jax.ShapeDtypeStruct((ROWS, D), F32),
        ],
        compiler_params=PARAMS,
        name="key%d" % s,
    )(at, *parts, cosine, sine)


def local(
    hidden,
    expert_ids,
    expert_gates,
    w_gate,
    w_up,
    w_down,
    w_latent,
    queries,
    cache,
    lengths,
    came_from,
):
    my_dp = lax.axis_index("dp")
    my_ep = lax.axis_index("ep")
    me = jnp.stack([my_dp, my_ep]).astype(jnp.int32)
    at = jnp.stack([my_ep // 2, my_ep % 2]).astype(jnp.int32)
    table, cosine, sine = make_table(me, came_from, lengths)
    qt = jnp.swapaxes(queries, 2, 3)
    cache_t = jnp.swapaxes(cache, 1, 2)
    latent_t = w_latent.T

    packed = pl.pallas_call(
        pack_kernel,
        in_specs=[VMEM] * 3,
        out_specs=VMEM,
        out_shape=jax.ShapeDtypeStruct((N_EP, 2 * ROWS, WIDE), BF16),
        compiler_params=PARAMS,
        name="pack",
    )(hidden, expert_ids, expert_gates)
    gathered = lax.all_to_all(packed, "ep", split_axis=0, concat_axis=0, tiled=True)
    out_shape = jax.ShapeDtypeStruct((N_DP, PER_DP, SLICE), BF16)
    sends = pl.pallas_call(
        dispatch_kernel,
        in_specs=[VMEM],
        out_specs=[VMEM, VMEM],
        out_shape=[out_shape, out_shape],
        compiler_params=PARAMS,
        name="dispatch",
    )(gathered)

    first_old = old0(table, qt, cache_t)

    arrived = [to_dp(sends[s]) for s in range(2)]
    keep, send = gate_up(at, arrived[0], w_gate, w_up, first_old[1], cosine)
    own0, parts0 = pair_sum(keep, send)
    second_old = old1(table, qt, cache_t, parts0[0])
    act0 = activate(own0, parts0)
    keep, send = gate_up(at, arrived[1], w_gate, w_up, second_old[1], act0)
    own1, parts1 = pair_sum(keep, send)
    pieces = cut_pieces(table, cache_t, arrived[1])
    spread = to_dp(pieces)
    result0 = finish(at, act0, w_down, spread)
    back0 = to_dp(result0)
    act1 = activate(own1, parts1)
    result1 = finish(at, act1, w_down, spread)
    back1 = to_dp(result1)
    key0, block0, mixed0 = make_keys(0, at, gathered, back0, latent_t, cosine[0], sine[0], table)
    onward = forward(table, spread.reshape(2 * N_DP, 144, 128), block0)
    attended = merge(0, table, qt, first_old, [key0], None)
    key1, _, mixed1 = make_keys(1, at, gathered, back1, latent_t, cosine[1], sine[1], onward)
    landed = to_dp(onward)
    attended = merge(1, table, qt, second_old, [key0, key1], attended)
    attended = moved_rows(table, qt, landed, key1, attended)
    expert_out = jnp.stack([mixed0, mixed1]).astype(BF16)
    return (expert_out, attended)


def solution(mesh):
    in_specs = (
        P(None, ("dp", "ep"), None),
        P(None, ("dp", "ep"), None),
        P(None, ("dp", "ep"), None),
        P("dp", "ep", None),
        P("dp", "ep", None),
        P("dp", None, "ep"),
        P("ep", None),
        P(None, ("dp", "ep"), None, None),
        P(("dp", "ep"), None, None),
        P(),
        P(),
    )
    out_specs = (P(None, ("dp", "ep"), None), P(None, ("dp", "ep"), None, None))
    return jax.shard_map(local, mesh=mesh, in_specs=in_specs, out_specs=out_specs, check_vma=False)
```

```python
import functools

import jax
import jax.numpy as jnp
import numpy as np
from jax import lax
from jax.experimental import pallas as pl
from jax.experimental.pallas import tpu as pltpu
from jax.sharding import PartitionSpec as P

F32 = jnp.float32
BF16 = jnp.bfloat16
D = 7168
LAT = 512
KV = 576
FF = 1024
EXPERTS = 32
CAP = 3
N_DP = 16
N_EP = 8
SLICE = D // N_EP
META = 128
WIDE = SLICE + META
ROWS = 8
TOPK = 8
SLOTS = EXPERTS * CAP * N_EP
PER_DP = SLOTS // N_DP
HALF = SLOTS // 2
KVW = 768
KEYW = 640
SCALE = 192.0 ** (-0.5)
EPS = 1e-06
VMEM = pl.BlockSpec(memory_space=pltpu.VMEM)
ANY = pl.BlockSpec(memory_space=pl.ANY)
PARAMS = pltpu.CompilerParams(vmem_limit_bytes=48 * 1024 * 1024)


FULL = pltpu.CompilerParams(vmem_limit_bytes=60 * 1024 * 1024)


def in_hbm(*shape):
    return pltpu.HBM(shape, BF16)


def whole(*shape):
    return pl.BlockSpec(shape, lambda *_: (0,) * len(shape))


def cost(flops, nbytes):
    return pl.CostEstimate(flops=int(flops), bytes_accessed=int(nbytes), transcendentals=0)


def split3(v):
    hi = v.astype(BF16).astype(F32)
    mid = (v - hi).astype(BF16).astype(F32)
    lo = (v - hi - mid).astype(BF16).astype(F32)
    return hi, mid, lo


def pack_kernel(hidden_ref, ids_ref, gates_ref, out_ref):
    lane = lax.broadcasted_iota(jnp.int32, (ROWS, META), 1)
    rows = []
    metas = []
    for s in range(2):
        h = hidden_ref[s].astype(F32)
        scale = lax.rsqrt(jnp.mean(h * h, axis=-1, keepdims=True) + EPS)
        ids = ids_ref[s].astype(F32)
        parts = split3(gates_ref[s])
        meta = jnp.zeros((ROWS, META), F32)
        for k in range(TOPK):
            meta = jnp.where(lane == k, ids[:, k : k + 1], meta)
            for n, part in enumerate(parts):
                meta = jnp.where(lane == 8 + 8 * n + k, part[:, k : k + 1], meta)
        for n, part in enumerate(split3(scale)):
            meta = jnp.where(lane == 32 + n, part, meta)
        rows.append(h)
        metas.append(meta)
    meta = jnp.concatenate(metas, axis=0).astype(BF16)
    for j in range(N_EP):
        cut = slice(j * SLICE, (j + 1) * SLICE)
        both = jnp.concatenate([rows[0][:, cut], rows[1][:, cut]], axis=0)
        out_ref[j, :, :SLICE] = both.astype(BF16)
        out_ref[j, :, SLICE:] = meta


def unpack(r_ref, s):
    rows = r_ref[...].astype(F32)[:, 8 * s : 8 * s + 8, :].reshape(N_EP * ROWS, WIDE)
    n = N_EP * ROWS
    hid = rows[:, :SLICE]
    meta = rows[:, SLICE:]
    mt = meta.T
    ids = mt[0:8]
    gates = mt[8:16] + mt[16:24] + mt[24:32]
    scale = meta[:, 32:33] + meta[:, 33:34] + meta[:, 34:35]
    expert = lax.broadcasted_iota(jnp.int32, (EXPERTS, n), 0).astype(F32)
    onehot = jnp.zeros((EXPERTS, n), F32)
    gm = jnp.zeros((EXPERTS, n), F32)
    for k in range(TOPK):
        eq = expert == ids[k : k + 1]
        onehot = jnp.where(eq, 1.0, onehot)
        gm = jnp.where(eq, gates[k : k + 1], gm)
    p = lax.broadcasted_iota(jnp.int32, (n, n), 0)
    q = lax.broadcasted_iota(jnp.int32, (n, n), 1)
    earlier = jnp.where(((p >> 3) == (q >> 3)) & (p < q), 1.0, 0.0).astype(BF16)
    rank = jnp.dot(onehot.astype(BF16), earlier, preferred_element_type=F32)
    b = lax.broadcasted_iota(jnp.int32, (N_EP, n), 0)
    qq = lax.broadcasted_iota(jnp.int32, (N_EP, n), 1)
    block = jnp.where((qq >> 3) == b, 1.0, 0.0)

    def place(values):
        pieces = []
        for r in range(CAP):
            picked = jnp.where((rank == float(r)) & (onehot > 0.0), values, 0.0)
            pieces.append((picked[:, None, :] * block[None, :, :])[:, None])
        return jnp.concatenate(pieces, axis=1).reshape(SLOTS, n)

    return hid, scale, onehot, gm, place


def dispatch_kernel(r_ref, out0_ref, out1_ref):
    for s, out_ref in enumerate((out0_ref, out1_ref)):
        hid, scale, onehot, _, place = unpack(r_ref, s)
        normed = (hid * scale).astype(BF16)
        table = place(onehot).astype(BF16)
        out = jnp.dot(table, normed, preferred_element_type=F32)
        out_ref[...] = out.reshape(N_DP, PER_DP, SLICE).astype(BF16)


def total(values, axis):
    return jnp.sum(values, axis=axis, keepdims=True)


def table_kernel(me_ref, from_ref, len_ref, freq_ref, tab_ref, cos_ref, sin_ref, hold_ref):
    n = N_DP * ROWS
    my_dp, my_ep = me_ref[0], me_ref[1]
    sub = lax.broadcasted_iota(jnp.int32, (n, n), 0)
    lane = lax.broadcasted_iota(jnp.int32, (n, n), 1)
    lane64 = lax.broadcasted_iota(jnp.int32, (n, 64), 1)
    sub64 = lax.broadcasted_iota(jnp.int32, (n, 64), 0)
    wanted = lane64 == my_ep * ROWS + (sub64 & 7)

    def column(ref):
        wide = jnp.broadcast_to(ref[...][:, None, :], (N_DP, ROWS, 64)).reshape(n, 64)
        return total(jnp.where(wanted, wide, 0), 1)

    def as_row(col):
        return total(jnp.where(sub == lane, col, 0), 0)

    came = column(from_ref)
    lens = column(len_ref)
    src_dp = came >> 6
    src = src_dp * ROWS + (came & 7)
    home = lax.broadcasted_iota(jnp.int32, (n, 1), 0)
    arriving = src_dp != (home >> 3)
    arriving_row = as_row(arriving.astype(jnp.int32))
    hit = src == lane
    away_row = total(jnp.where(hit & arriving, 1, 0), 0)
    label = total(jnp.where(((src >> 3) == (lane >> 3)) & (lane < src), away_row, 0), 1)
    turn = total(jnp.where(((sub >> 3) == (lane >> 3)) & (lane < sub), arriving_row, 0), 1)
    second = total(jnp.where(hit, as_row(lens), 0), 1)
    mine = sub == my_dp * ROWS + lane
    here = ((sub >> 3) == my_dp) & arriving & (turn == lane)
    onward = ((sub >> 3) == (lane >> 1)) & arriving & (turn == (lane & 1)) & (lane < 2 * N_DP)
    gone = ((src >> 3) == my_dp) & arriving & (label == lane)
    lane_row = lax.broadcasted_iota(jnp.int32, (1, n), 1)
    spot = jnp.where(lane_row == 0, my_ep >> 1, jnp.where(lane_row == 1, my_ep & 1, 0))
    rows = [
        total(jnp.where(mine, second, 0), 0),
        total(jnp.where(mine & ~arriving, src & 7, 0), 0),
        total(jnp.where(here, src, 0), 0),
        total(jnp.where(here, home & 7, 0), 0),
        total(jnp.where(onward, src_dp * 2 + label, 0), 0),
        total(jnp.where(gone, src & 7, 0), 0),
        total(jnp.where(mine, lens, 0), 0),
        spot,
    ]
    tab_ref[...] = jnp.concatenate(rows, axis=0)
    hold_ref[0] = lens.astype(F32)
    hold_ref[1] = (second + 1).astype(F32)
    live = lax.broadcasted_iota(jnp.int32, (ROWS, 128), 1) < 64
    for s in range(2):
        angle = hold_ref[s, pl.ds(pl.multiple_of(my_dp * ROWS, ROWS), ROWS), :] * freq_ref[...]
        cos_ref[s] = jnp.where(live, jnp.cos(angle), 0.0)
        sin_ref[s] = jnp.where(live, jnp.sin(angle), 0.0)


def make_table(me, came_from, lengths):
    freq = jnp.asarray(np.tile(10000.0 ** (-2.0 * np.arange(32) / 64), 4)[None], F32)
    wave = jax.ShapeDtypeStruct((2, ROWS, 128), F32)
    return pl.pallas_call(
        table_kernel,
        in_specs=[pl.BlockSpec(memory_space=pltpu.SMEM)] + [VMEM] * 3,
        out_specs=[VMEM] * 3,
        out_shape=[jax.ShapeDtypeStruct((8, 128), jnp.int32), wave, wave],
        scratch_shapes=[pltpu.VMEM((2, N_DP * ROWS, 1), F32)],
        compiler_params=PARAMS,
        name="table",
    )(me, came_from.reshape(N_DP, 64), lengths.reshape(N_DP, 64), freq)


def gateup_kernel(at_ref, x_ref, wg_ref, wu_ref, after_ref, also_ref, keep_ref, send_ref):
    core = at_ref[1]
    for e in range(2):
        lhs = x_ref[:, 16 * e : 16 * e + 32, :].reshape(N_DP * 32, SLICE)
        halves = []
        for w_ref in (wg_ref, wu_ref):
            full = jnp.dot(lhs, w_ref[e], preferred_element_type=F32)
            full = full.reshape(N_DP, 32, 256)[:, 8 * e : 8 * e + 24, :].reshape(HALF, 256)
            halves.append((full[:, :128], full[:, 128:]))
        (g0, g1), (u0, u1) = halves
        first = core == 0
        keep_ref[0, e, :, :128] = jnp.where(first, g0, g1).astype(BF16)
        keep_ref[0, e, :, 128:] = jnp.where(first, u0, u1).astype(BF16)
        send_ref[0, e, :, :128] = jnp.where(first, g1, g0).astype(BF16)
        send_ref[0, e, :, 128:] = jnp.where(first, u1, u0).astype(BF16)


def gate_up(at, x, w_gate, w_up, after, also):
    wspec = pl.BlockSpec((2, SLICE, 256), lambda r, a: (0, 0, (a[0] + r) % 4))
    ospec = pl.BlockSpec((1, 2, HALF, 256), lambda r, a: (r, 0, 0, 0))
    shape = jax.ShapeDtypeStruct((4, 2, HALF, 256), BF16)
    return pl.pallas_call(
        gateup_kernel,
        grid_spec=pltpu.PrefetchScalarGridSpec(
            num_scalar_prefetch=1,
            grid=(4,),
            in_specs=[
                pl.BlockSpec((N_DP, PER_DP, SLICE), lambda r, a: (0, 0, 0)),
                wspec,
                wspec,
                ANY,
                ANY,
            ],
            out_specs=[ospec, ospec],
        ),
        out_shape=[shape, shape],
        compiler_params=PARAMS,
        cost_estimate=cost(4e9, 12e6),
        name="gate_up",
    )(at, x, w_gate, w_up, after, also)


def down_kernel(at_ref, *refs):
    acts = refs[:8]
    w_ref = refs[8]
    out_ref = refs[-1]
    x = at_ref[0]
    first = at_ref[1] == 0
    results = []
    for e in range(2):
        total = jnp.zeros((HALF, SLICE), F32)
        for n, shift in enumerate((0, 3, 1, 2)):
            own = acts[n][e]
            other = acts[4 + n][e]
            low = jnp.where(first, own, other)
            high = jnp.where(first, other, own)
            lhs = jnp.concatenate([low, high], axis=1)
            chip = (x + shift) & 3
            rhs = w_ref[e, pl.ds(pl.multiple_of(chip * 256, 256), 256), :]
            total = total + jnp.dot(lhs, rhs, preferred_element_type=F32)
        results.append(total.reshape(N_DP, PER_DP // 2, SLICE))
    out_ref[...] = jnp.concatenate(results, axis=1).astype(BF16)


def down(at, acts, w_down, after):
    return pl.pallas_call(
        down_kernel,
        grid=(1,),
        in_specs=[pl.BlockSpec(memory_space=pltpu.SMEM)]
        + [whole(2, HALF, 128)] * 8
        + [whole(2, FF, SLICE), ANY],
        out_specs=whole(N_DP, PER_DP, SLICE),
        out_shape=in_hbm(N_DP, PER_DP, SLICE),
        compiler_params=FULL,
        cost_estimate=cost(2e9, 8e6),
        name="down",
    )(at, *acts, w_down, after)


def combine_kernel(s, at_ref, r_ref, ret_ref, wl_ref, after_ref, own_ref, other_ref, all_ref):
    hid, _, _, gm, place = unpack(r_ref, s)
    weights = place(gm)
    high = weights.astype(BF16)
    low = (weights - high.astype(F32)).astype(BF16)
    ret = ret_ref[...].reshape(SLOTS, SLICE)
    dims = (((0,), (0,)), ((), ()))
    mixed = lax.dot_general(high, ret, dims, preferred_element_type=F32)
    mixed = mixed + lax.dot_general(low, ret, dims, preferred_element_type=F32)
    resid = hid + mixed
    square = jnp.sum(resid * resid, axis=-1, keepdims=True)
    kv = lax.dot_general(
        resid.astype(BF16), wl_ref[...], (((1,), (1,)), ((), ())), preferred_element_type=F32
    )
    all_ref[:, :, :KV] = kv.reshape(N_EP, ROWS, KV)
    all_ref[:, :, KEYW:KVW] = jnp.broadcast_to(square, (N_EP * ROWS, KVW - KEYW)).reshape(
        N_EP, ROWS, KVW - KEYW
    )
    all_ref[:, :, KV:KEYW] = jnp.zeros((N_EP, ROWS, KEYW - KV), F32)
    all_ref[:, :, KVW:] = mixed.reshape(N_EP, ROWS, SLICE)
    for r in range(4):
        base = 2 * ((at_ref[0] - r) & 3)
        own_ref[r] = all_ref[base + at_ref[1]]
        other_ref[r] = all_ref[base + 1 - at_ref[1]]


def fold_kernel(own_ref, got_ref, *out_refs):
    for r, out_ref in enumerate(out_refs):
        out_ref[:, :KVW] = own_ref[r, :, :KVW] + got_ref[r, :, :KVW]
        out_ref[:, KVW : KVW + SLICE] = own_ref[r, :, KVW:]
        out_ref[:, KVW + SLICE :] = got_ref[r, :, KVW:]


def key_kernel(at_ref, u0_ref, u1_ref, u2_ref, u3_ref, cos_ref, sin_ref, key_ref, block_ref, mixed_ref):
    parts = (u0_ref, u1_ref, u2_ref, u3_ref)
    kv = sum(u[:, :KVW] for u in parts)
    core = at_ref[1]
    for r, u in enumerate(parts):
        chip = (at_ref[0] + r) & 3
        for which, j in enumerate((2 * chip + core, 2 * chip + 1 - core)):
            lanes = pl.ds(pl.multiple_of(j * SLICE, SLICE), SLICE)
            cut = slice(KVW + which * SLICE, KVW + (which + 1) * SLICE)
            mixed_ref[:, lanes] = u[:, cut]
    raw = kv[:, :KEYW] * lax.rsqrt(kv[:, KEYW : KEYW + 1] * (1.0 / D) + EPS)
    latent = raw[:, :LAT]
    latent = latent * lax.rsqrt(jnp.mean(latent * latent, axis=-1, keepdims=True) + EPS)
    part = raw[:, LAT:]
    lane = lax.broadcasted_iota(jnp.int32, part.shape, 1)
    turned = jnp.where(lane < 32, -pltpu.roll(part, 96, 1), pltpu.roll(part, 32, 1))
    rotated = part * cos_ref[...] + turned * sin_ref[...]
    key = jnp.concatenate([latent, rotated], axis=1)
    key_ref[...] = key.astype(BF16).astype(F32)
    tiles = [key[:, 128 * n : 128 * n + 128] for n in range(5)] + [jnp.zeros((ROWS, 128), F32)]
    block_ref[...] = jnp.concatenate(tiles, axis=0).astype(BF16)


def old_attention(q, kt, count):
    scores = lax.dot_general(q, kt, (((0,), (0,)), ((), ())), preferred_element_type=F32) * SCALE
    lane = lax.broadcasted_iota(jnp.int32, scores.shape, 1)
    valid = lane < count
    scores = jnp.where(valid, scores, -1e30)
    top = jnp.max(scores, axis=1, keepdims=True)
    weights = jnp.where(valid, jnp.exp(scores - top), 0.0)
    total = jnp.sum(weights, axis=1, keepdims=True)
    out = lax.dot_general(
        weights.astype(BF16), kt[:LAT], (((1,), (1,)), ((), ())), preferred_element_type=F32
    )
    return out, top, total


def store_old(out_ref, stat_ref, parts):
    out, top, total = parts
    lane = lax.broadcasted_iota(jnp.int32, (128, 128), 1)
    out_ref[0] = out
    stat_ref[0] = jnp.where(lane == 0, top, total)


def old0_kernel(len_ref, q_ref, kt_ref, out_ref, stat_ref):
    count = len_ref[6, pl.program_id(0)]
    store_old(out_ref, stat_ref, old_attention(q_ref[0, 0], kt_ref[0], count))


def old1_kernel(tab_ref, q_ref, kt_ref, after_ref, out_ref, stat_ref):
    count = tab_ref[0, pl.program_id(0)]
    store_old(out_ref, stat_ref, old_attention(q_ref[0, 0], kt_ref[0], count))


OLD_SHAPE = [
    jax.ShapeDtypeStruct((ROWS, 128, LAT), F32),
    jax.ShapeDtypeStruct((ROWS, 128, 128), F32),
]
OLD_SPECS = [
    pl.BlockSpec((1, 128, LAT), lambda t, a: (t, 0, 0)),
    pl.BlockSpec((1, 128, 128), lambda t, a: (t, 0, 0)),
]


def old0(lens, qt, cache_t):
    return pl.pallas_call(
        old0_kernel,
        grid_spec=pltpu.PrefetchScalarGridSpec(
            num_scalar_prefetch=1,
            grid=(ROWS,),
            in_specs=[
                pl.BlockSpec((1, 1, KV, 128), lambda t, a: (0, t, 0, 0)),
                pl.BlockSpec((1, KV, 512), lambda t, a: (t, 0, 0)),
            ],
            out_specs=OLD_SPECS,
        ),
        out_shape=OLD_SHAPE,
        compiler_params=PARAMS,
        cost_estimate=cost(5e9, 8e6),
        name="old0",
    )(lens, qt, cache_t)


def old1(table, qt, cache_t, after):
    return pl.pallas_call(
        old1_kernel,
        grid_spec=pltpu.PrefetchScalarGridSpec(
            num_scalar_prefetch=1,
            grid=(ROWS,),
            in_specs=[
                pl.BlockSpec((1, 1, KV, 128), lambda t, a: (1, t, 0, 0)),
                pl.BlockSpec((1, KV, 512), lambda t, a: (a[1, t], 0, 0)),
                ANY,
            ],
            out_specs=OLD_SPECS,
        ),
        out_shape=OLD_SHAPE,
        compiler_params=PARAMS,
        cost_estimate=cost(5e9, 8e6),
        name="old1",
    )(table, qt, cache_t, after)


def add_new(q, old, keys):
    out, top, total = old
    lane = lax.broadcasted_iota(jnp.int32, (128, ROWS), 1)
    sub = lax.broadcasted_iota(jnp.int32, (ROWS, LAT), 0)
    scores = []
    values = []
    for key, row in keys:
        both = jnp.dot(key[:, :KV].astype(BF16), q, preferred_element_type=F32).T
        scores.append(jnp.sum(jnp.where(lane == row, both, 0.0), axis=1, keepdims=True) * SCALE)
        values.append(jnp.sum(jnp.where(sub == row, key[:, :LAT], 0.0), axis=0, keepdims=True))
    peak = top
    for s in scores:
        peak = jnp.maximum(peak, s)
    shrink = jnp.exp(top - peak)
    out = out * shrink
    total = total * shrink
    for s, v in zip(scores, values):
        w = jnp.exp(s - peak)
        total = total + w
        out = out + w * v
    return (out / total).astype(BF16)


def merge_kernel(step, tab_ref, q_ref, old_ref, stat_ref, *refs):
    out_ref = refs[-1]
    t = pl.program_id(0)
    if step == 0:
        keys = [(refs[0][...], t)]
    else:
        keys = [(refs[0][...], tab_ref[1, t]), (refs[1][...], t)]
    old = (old_ref[0], stat_ref[0, :, 0:1], stat_ref[0, :, 1:2])
    out_ref[0, 0] = add_new(q_ref[0, 0], old, keys)


def merge(step, table, qt, old, keys, buffer):
    in_specs = [
        pl.BlockSpec((1, 1, KV, 128), lambda t, a: (step, t, 0, 0)),
        pl.BlockSpec((1, 128, LAT), lambda t, a: (t, 0, 0)),
        pl.BlockSpec((1, 128, 128), lambda t, a: (t, 0, 0)),
    ] + [pl.BlockSpec((ROWS, KEYW), lambda t, a: (0, 0))] * len(keys)
    args = [table, qt, *old, *keys]
    alias = {}
    if buffer is not None:
        in_specs.append(ANY)
        alias = {len(args): 0}
        args.append(buffer)
    return pl.pallas_call(
        functools.partial(merge_kernel, step),
        grid_spec=pltpu.PrefetchScalarGridSpec(
            num_scalar_prefetch=1,
            grid=(ROWS,),
            in_specs=in_specs,
            out_specs=pl.BlockSpec((1, 1, 128, LAT), lambda t, a: (step, t, 0, 0)),
        ),
        out_shape=jax.ShapeDtypeStruct((2, ROWS, 128, LAT), BF16),
        input_output_aliases=alias,
        compiler_params=PARAMS,
        cost_estimate=cost(1e8, 5e6),
        name="merge%d" % step,
    )(*args)


def moved_kernel(tab_ref, q_ref, kv_ref, keys_ref, key1_ref, buffer_ref, out_ref, kt_ref):
    k = pl.program_id(0)
    slot = tab_ref[3, k]
    for j in range(N_DP):
        f, l = j // 4, j % 4
        kt_ref[144 * f : 144 * f + 144, 128 * l : 128 * l + 128] = kv_ref[j]
    raw = keys_ref[...].astype(F32)
    where = tab_ref[2, k]
    pick = lax.broadcasted_iota(jnp.int32, (N_DP, ROWS, 1), 0) * ROWS
    pick = pick + lax.broadcasted_iota(jnp.int32, (N_DP, ROWS, 1), 1)
    rows = []
    for n in range(5):
        tile = jnp.where(pick == where, raw[:, 8 * n : 8 * n + 8, :], 0.0)
        rows.append(jnp.sum(jnp.sum(tile, axis=0), axis=0, keepdims=True))
    first = jnp.broadcast_to(jnp.concatenate(rows, axis=1), (ROWS, KEYW))
    q = q_ref[0, 0]
    old = old_attention(q, kt_ref[...], tab_ref[0, slot])
    out_ref[0, 0] = add_new(q, old, [(first, 0), (key1_ref[...], slot)])


def moved_rows(table, qt, landed, key1, buffer):
    return pl.pallas_call(
        moved_kernel,
        grid_spec=pltpu.PrefetchScalarGridSpec(
            num_scalar_prefetch=1,
            grid=(2,),
            in_specs=[
                pl.BlockSpec((1, 1, KV, 128), lambda k, a: (1, a[3, k], 0, 0)),
                pl.BlockSpec((N_DP, 144, 128), lambda k, a: (0, k, 0)),
                pl.BlockSpec((N_DP, 48, 128), lambda k, a: (0, 6, 0)),
                pl.BlockSpec((ROWS, KEYW), lambda k, a: (0, 0)),
                ANY,
            ],
            out_specs=pl.BlockSpec((1, 1, 128, LAT), lambda k, a: (1, a[3, k], 0, 0)),
            scratch_shapes=[pltpu.VMEM((KV, 512), BF16)],
        ),
        out_shape=jax.ShapeDtypeStruct((2, ROWS, 128, LAT), BF16),
        input_output_aliases={5: 0},
        compiler_params=PARAMS,
        cost_estimate=cost(6e8, 3e6),
        name="moved_rows",
    )(table, qt, landed, landed, key1, buffer)


def run_copies(copies):
    for c in copies:
        c.start()
    for c in copies:
        c.wait()


def cut_kernel(leaving_ref, cache_ref, after_ref, out_ref, sem):
    copies = []
    for q in range(2):
        row = leaving_ref[5, q]
        for j in range(N_DP):
            f, l = j // 4, j % 4
            src = cache_ref.at[row, pl.ds(144 * f, 144), pl.ds(128 * l, 128)]
            copies.append(pltpu.make_async_copy(src, out_ref.at[j, q], sem.at[q * N_DP + j]))
    run_copies(copies)


def cut_pieces(leaving, cache_t, after):
    return pl.pallas_call(
        cut_kernel,
        in_specs=[pl.BlockSpec(memory_space=pltpu.SMEM), ANY, ANY],
        out_specs=VMEM,
        out_shape=jax.ShapeDtypeStruct((N_DP, 2, 144, 128), BF16),
        scratch_shapes=[pltpu.SemaphoreType.DMA((2 * N_DP,))],
        compiler_params=PARAMS,
        cost_estimate=cost(1e6, 3e6),
        name="cut_pieces",
    )(leaving, cache_t, after)


def forward_kernel(idx_ref, src_ref, key_ref, out_ref, sem):
    copies = []
    for d in range(N_DP):
        for k in range(2):
            n = 2 * d + k
            dst = out_ref.at[d, pl.ds(144 * k, 144)]
            copies.append(pltpu.make_async_copy(src_ref.at[idx_ref[4, n]], dst, sem.at[n]))
        dst = out_ref.at[d, pl.ds(288, 48)]
        copies.append(pltpu.make_async_copy(key_ref, dst, sem.at[2 * N_DP + d]))
    run_copies(copies)


def forward(idx, pieces, key_block):
    return pl.pallas_call(
        forward_kernel,
        in_specs=[pl.BlockSpec(memory_space=pltpu.SMEM), VMEM, VMEM],
        out_specs=VMEM,
        out_shape=jax.ShapeDtypeStruct((N_DP, 336, 128), BF16),
        scratch_shapes=[pltpu.SemaphoreType.DMA((3 * N_DP,))],
        compiler_params=PARAMS,
        cost_estimate=cost(1e6, 3e6),
        name="forward",
    )(idx, pieces, key_block)


SIB = [(i, i ^ 1) for i in range(8)]
XP = [(i, (i + 2) % 8) for i in range(8)]
XM = [(i, (i - 2) % 8) for i in range(8)]
X2 = [(i, (i + 4) % 8) for i in range(8)]


def to_dp(v):
    return lax.all_to_all(v, "dp", split_axis=0, concat_axis=0, tiled=True)


def hop(v, pairs):
    return lax.ppermute(v, "ep", pairs)


def pair_sum(keep, send):
    got = hop(send, SIB)
    parts = [(keep[r].astype(F32) + got[r].astype(F32)).astype(BF16) for r in (1, 2, 3)]
    return keep[0].astype(F32) + got[0].astype(F32), parts


def activate(own, parts):
    a1 = hop(parts[0], XP)
    a2 = hop(parts[1], X2)
    a3 = hop(parts[2], XM)
    total = own + a1.astype(F32) + a2.astype(F32) + a3.astype(F32)
    return (jax.nn.silu(total[..., :128]) * total[..., 128:]).astype(BF16)


def finish(at, act, w_down, after):
    b1 = hop(act, XP)
    b3 = hop(act, XM)
    b2 = hop(act, X2)
    ours = [act, b1, b3, b2]
    theirs = [hop(v, SIB) for v in ours]
    return down(at, ours + theirs, w_down, after)


def make_keys(s, at, gathered, returned, latent_t, cosine, sine, after):
    smem = pl.BlockSpec(memory_space=pltpu.SMEM)
    width = KVW + SLICE
    shape = jax.ShapeDtypeStruct((4, ROWS, width), F32)
    own, other = pl.pallas_call(
        functools.partial(combine_kernel, s),
        in_specs=[smem, VMEM, VMEM, VMEM, ANY],
        out_specs=[VMEM, VMEM],
        out_shape=[shape, shape],
        scratch_shapes=[pltpu.VMEM((N_EP, ROWS, width), F32)],
        compiler_params=PARAMS,
        cost_estimate=cost(4e8, 4e6),
        name="combine%d" % s,
    )(at, gathered, returned, latent_t, after)
    got = hop(other, SIB)
    shape = jax.ShapeDtypeStruct((ROWS, width + SLICE), F32)
    sums = pl.pallas_call(
        fold_kernel,
        in_specs=[VMEM, VMEM],
        out_specs=[VMEM] * 4,
        out_shape=[shape] * 4,
        compiler_params=PARAMS,
        name="fold%d" % s,
    )(own, got)
    parts = [sums[0], hop(sums[1], XM), hop(sums[2], X2), hop(sums[3], XP)]
    return pl.pallas_call(
        key_kernel,
        in_specs=[smem] + [VMEM] * 6,
        out_specs=[VMEM] * 3,
        out_shape=[
            jax.ShapeDtypeStruct((ROWS, KEYW), F32),
            jax.ShapeDtypeStruct((48, 128), BF16),
            jax.ShapeDtypeStruct((ROWS, D), F32),
        ],
        compiler_params=PARAMS,
        name="key%d" % s,
    )(at, *parts, cosine, sine)


def local(
    hidden,
    expert_ids,
    expert_gates,
    w_gate,
    w_up,
    w_down,
    w_latent,
    queries,
    cache,
    lengths,
    came_from,
):
    my_dp = lax.axis_index("dp")
    my_ep = lax.axis_index("ep")
    me = jnp.stack([my_dp, my_ep]).astype(jnp.int32)
    at = jnp.stack([my_ep // 2, my_ep % 2]).astype(jnp.int32)
    table, cosine, sine = make_table(me, came_from, lengths)
    qt = jnp.swapaxes(queries, 2, 3)
    cache_t = jnp.swapaxes(cache, 1, 2)
    latent_t = w_latent.T

    packed = pl.pallas_call(
        pack_kernel,
        grid=(1,),
        in_specs=[whole(2, ROWS, D), whole(2, ROWS, TOPK), whole(2, ROWS, TOPK)],
        out_specs=whole(N_EP, 2 * ROWS, WIDE),
        out_shape=in_hbm(N_EP, 2 * ROWS, WIDE),
        compiler_params=FULL,
        name="pack",
    )(hidden, expert_ids, expert_gates)
    gathered = lax.all_to_all(packed, "ep", split_axis=0, concat_axis=0, tiled=True)
    out_shape = in_hbm(N_DP, PER_DP, SLICE)
    sends = pl.pallas_call(
        dispatch_kernel,
        grid=(1,),
        in_specs=[whole(N_EP, 2 * ROWS, WIDE)],
        out_specs=[whole(N_DP, PER_DP, SLICE)] * 2,
        out_shape=[out_shape, out_shape],
        compiler_params=FULL,
        name="dispatch",
    )(gathered)

    first_old = old0(table, qt, cache_t)

    arrived = [to_dp(sends[s]) for s in range(2)]
    keep, send = gate_up(at, arrived[0], w_gate, w_up, first_old[1], cosine)
    own0, parts0 = pair_sum(keep, send)
    second_old = old1(table, qt, cache_t, parts0[0])
    act0 = activate(own0, parts0)
    keep, send = gate_up(at, arrived[1], w_gate, w_up, second_old[1], act0)
    own1, parts1 = pair_sum(keep, send)
    pieces = cut_pieces(table, cache_t, arrived[1])
    spread = to_dp(pieces)
    result0 = finish(at, act0, w_down, spread)
    back0 = to_dp(result0)
    act1 = activate(own1, parts1)
    result1 = finish(at, act1, w_down, spread)
    back1 = to_dp(result1)
    key0, block0, mixed0 = make_keys(0, at, gathered, back0, latent_t, cosine[0], sine[0], table)
    onward = forward(table, spread.reshape(2 * N_DP, 144, 128), block0)
    attended = merge(0, table, qt, first_old, [key0], None)
    key1, _, mixed1 = make_keys(1, at, gathered, back1, latent_t, cosine[1], sine[1], onward)
    landed = to_dp(onward)
    attended = merge(1, table, qt, second_old, [key0, key1], attended)
    attended = moved_rows(table, qt, landed, key1, attended)
    expert_out = jnp.stack([mixed0, mixed1]).astype(BF16)
    return (expert_out, attended)


def solution(mesh):
    in_specs = (
        P(None, ("dp", "ep"), None),
        P(None, ("dp", "ep"), None),
        P(None, ("dp", "ep"), None),
        P("dp", "ep", None),
        P("dp", "ep", None),
        P("dp", None, "ep"),
        P("ep", None),
        P(None, ("dp", "ep"), None, None),
        P(("dp", "ep"), None, None),
        P(),
        P(),
    )
    out_specs = (P(None, ("dp", "ep"), None), P(None, ("dp", "ep"), None, None))
    return jax.shard_map(local, mesh=mesh, in_specs=in_specs, out_specs=out_specs, check_vma=False)
```
